128 devices in a mesh: cam: 8 (over x, core), band: 16 (over z, y).
Axes of the slice: x: 4, y: 4, z: 4, core: 2. Of those that a mesh axis runs over, the one named last changes fastest.
Arguments:
- query: bfloat16 [65536, 256], P(('cam', 'band')), may hold values from -6 to 6
- key_img: bfloat16 [8, 16384, 256], P('cam', 'band'), may hold values from -6 to 6
- value_img: bfloat16 [8, 16384, 256], P('cam', 'band'), may hold values from -6 to 6
- d_out: bfloat16 [65536, 256], P(('cam', 'band')), may hold values from -12 to 12
- visible: int32 [128, 6], replicated, may hold values from 0 to 255, as said below
Outputs:
- d_query: bfloat16 [65536, 256], P(('cam', 'band'))
- d_key: bfloat16 [8, 16384, 256], P('cam', 'band')
- d_value: bfloat16 [8, 16384, 256], P('cam', 'band')
The draws below stay inside these ranges and needn't reach their ends.
Inputs may be any that keep to these rules, and one draw needn't show every extreme that they name: `visible`: row t names 6 different blocks, each of camera t // 16 or of camera (t // 16 + 1) mod 8, and at most one block of each row band.
All inputs are finite; a program needn't handle non-finite values.
Results may differ from the reference program's by a relative error of at most 0.013.
The reference program's roundings to bfloat16 on the way (of `tile_keys`, `probs_low` and `dscore`) count: a program that leaves them out, or rounds other values in their place, can miss the bound.
Values may be sent and summed in bfloat16 or wider, within the bound.
A program may use at most 192 MiB of HBM per device.

```python
import jax
import jax.numpy as jnp
from jax import lax

D = 256
HEADS = 8
HEAD_DIM = 32
BLOCK = 512
BLK_DEV = 2
TILE_Q = 512
VIS = 6
CAMS = 8
BANDS = 16
TILES = 128
IMG_ROWS = 16384


def draw_query(key, part):
    key = jax.random.fold_in(key, 11)
    row_count = TILES * TILE_Q
    field = jnp.clip(jax.random.normal(key, (row_count, D), jnp.float32), -4.0, 4.0)
    return field.astype(jnp.bfloat16)


def draw_key_img(key, part):
    key = jax.random.fold_in(key, 23)
    field = jnp.clip(1.5 * jax.random.normal(key, (CAMS, IMG_ROWS, D), jnp.float32), -6.0, 6.0)
    return field.astype(jnp.bfloat16)


def draw_visible(key, part):
    key = jax.random.fold_in(key, 5)
    key_jitter, key_offset, key_block = jax.random.split(key, 3)
    tile_ids = jnp.arange(TILES)
    camera = tile_ids // BANDS
    band_ids = jnp.arange(BANDS)
    preference = (BANDS - jnp.abs(2 * band_ids + 1 - BANDS)) * 48 // BANDS
    jitter_score = jax.random.randint(key_jitter, (TILES, BANDS), 0, 64)
    ranked_score = (jitter_score + preference[None, :]) * BANDS + band_ids[None, :]
    ranking = jnp.argsort(-ranked_score, axis=1, stable=True)
    chosen = ranking[:, :VIS]
    offset = jax.random.randint(key_offset, (TILES, VIS), 0, 2)
    block_pick = jax.random.randint(key_block, (TILES, VIS), 0, BLK_DEV)
    block_ids = ((camera[:, None] + offset) % CAMS * BANDS + chosen) * BLK_DEV + block_pick
    return block_ids.astype(jnp.int32)


def steps_of(own_key, extent, shards, least, top_value):
    def one(dim, shards_of):
        draws = jax.random.uniform(jax.random.fold_in(jax.random.fold_in(own_key, 6), dim), (shards_of,), jnp.float32, least / len(shards), top_value / len(shards))
        return jnp.repeat(jnp.exp(draws), extent[dim] // shards_of).reshape((-1,) + (1,) * (len(extent) - dim - 1))

    factor_of = one(*shards[0])
    for cut in shards[1:]:
        factor_of = factor_of * one(*cut)
    return factor_of


def scatter_about(key, dims, deviation, reach, cuts=(), held_as=jnp.bfloat16):
    level = steps_of(key, dims, cuts, -0.22, 0.18) if cuts else 1.0
    drawn = jax.random.normal(key, dims, jnp.float32) * deviation * level
    return jnp.minimum(jnp.maximum(drawn, -reach), reach).astype(held_as)


def setup_inputs(seed: int = 0) -> dict:
    keys = jax.random.split(jax.random.key(seed), 6)
    return {
        "query": draw_query(jax.random.fold_in(keys[5], 71), 0),
        "key_img": draw_key_img(jax.random.fold_in(keys[5], 71), 0),
        "value_img": scatter_about(keys[2], (CAMS, IMG_ROWS, D), 1.0, 6.0, ((0, 8), (1, 16))),
        "d_out": scatter_about(keys[3], (TILES * TILE_Q, D), 2.0, 12.0, ((0, 128),)),
        "visible": draw_visible(jax.random.fold_in(keys[5], 71), 0),
    }


def tile_grads(queries, grads_out, tile_keys, tile_values):
    row_count = queries.shape[0]
    scaling = HEAD_DIM ** -0.5
    query_f32 = queries.astype(jnp.float32).reshape(row_count, HEADS, HEAD_DIM)
    grads_f32 = grads_out.astype(jnp.float32).reshape(row_count, HEADS, HEAD_DIM)
    keys_f32 = tile_keys.astype(jnp.float32).reshape(-1, HEADS, HEAD_DIM)
    values_f32 = tile_values.astype(jnp.float32).reshape(-1, HEADS, HEAD_DIM)
    scores = jnp.einsum("qhd,khd->hqk", query_f32, keys_f32) * scaling
    row_max = jnp.max(scores, axis=-1, keepdims=True)
    logsum = row_max + jnp.log(jnp.sum(jnp.exp(scores - row_max), axis=-1, keepdims=True))
    probs = jnp.exp(scores - logsum)
    probs_low = lax.optimization_barrier(probs.astype(jnp.bfloat16)).astype(jnp.float32)
    attended = jnp.einsum("hqk,khd->qhd", probs_low, values_f32)
    delta = jnp.sum(grads_f32 * attended, axis=-1).T[..., None]
    dprob = jnp.einsum("qhd,khd->hqk", grads_f32, values_f32)
    dscore = lax.optimization_barrier((probs * (dprob - delta)).astype(jnp.bfloat16)).astype(jnp.float32)
    grad_query = (jnp.einsum("hqk,khd->qhd", dscore, keys_f32) * scaling).astype(jnp.bfloat16)
    grad_key = jnp.einsum("hqk,qhd->khd", dscore, query_f32) * scaling
    grad_value = jnp.einsum("hqk,qhd->khd", probs_low, grads_f32)
    return grad_query.reshape(row_count, D), grad_key.reshape(VIS, BLOCK, D), grad_value.reshape(VIS, BLOCK, D)


def reference(query, key_img, value_img, d_out, visible):
    block_total = CAMS * BANDS * BLK_DEV
    key_blocks = key_img.reshape(block_total, BLOCK, D)
    value_blocks = value_img.reshape(block_total, BLOCK, D)
    query_tiles = query.reshape(TILES, TILE_Q, D)
    grad_tiles = d_out.reshape(TILES, TILE_Q, D)

    def step(totals, inputs):
        tile_query, tile_grad, block_ids = inputs
        block_ids = block_ids.astype(jnp.int32)
        tile_keys = jnp.take(key_blocks, block_ids, axis=0).reshape(VIS * BLOCK, D)
        tile_values = jnp.take(value_blocks, block_ids, axis=0).reshape(VIS * BLOCK, D)
        grad_query, grad_key, grad_value = tile_grads(tile_query, tile_grad, tile_keys, tile_values)
        sum_keys = totals[0].at[block_ids].add(grad_key)
        sum_values = totals[1].at[block_ids].add(grad_value)
        return (sum_keys, sum_values), grad_query

    zero_grads = jnp.zeros((block_total, BLOCK, D), jnp.float32)
    (sum_keys, sum_values), grad_queries = lax.scan(step, (zero_grads, zero_grads), (query_tiles, grad_tiles, visible))
    d_query = grad_queries.reshape(TILES * TILE_Q, D)
    d_key = sum_keys.astype(jnp.bfloat16).reshape(CAMS, IMG_ROWS, D)
    d_value = sum_values.astype(jnp.bfloat16).reshape(CAMS, IMG_ROWS, D)
    return (d_query, d_key, d_value)
```

```python
import functools

import jax
import jax.numpy as jnp
from jax import lax
from jax.experimental import pallas as pl
from jax.experimental.pallas import tpu as pltpu
from jax.sharding import PartitionSpec as P

HEADS = 8
BLOCK = 512
VIS = 6
HEAD_DIM = 32
TILES = 8
SCALE = HEAD_DIM**-0.5
LOG2E = 1.4426950408889634
ROWS = 256
bf16 = jnp.bfloat16
f32 = jnp.float32


def dot(a, b, contract_a, contract_b):
    return lax.dot_general(
        a, b, (((contract_a,), (contract_b,)), ((), ())), preferred_element_type=f32
    )


def two_parts(x):
    high = x.astype(bf16)
    return jnp.concatenate([high, (x - high.astype(f32)).astype(bf16)], axis=0)


def fold(x):
    return functools.reduce(jnp.add, [x[:, i : i + 128] for i in range(0, x.shape[1], 128)])


def fold_max(x):
    return functools.reduce(jnp.maximum, [x[:, i : i + 128] for i in range(0, x.shape[1], 128)])


def head_kernel(ids, kt, vt, qt, gt, dqt, dkt, dvt, s_ref, e_ref, dp_ref, ds_ref):
    dkt[...] = jnp.zeros_like(dkt)
    dvt[...] = jnp.zeros_like(dvt)

    def tile(t, _):
        q_t, g_t = qt[t], gt[t]
        q = q_t.astype(f32).T.astype(bf16)
        g = g_t.astype(f32).T.astype(bf16)
        for r in range(0, BLOCK, ROWS):
            rows = slice(r, r + ROWS)
            top = None
            for j in range(VIS):
                s = dot(q[rows], kt[ids[t, j]], 1, 0)
                s_ref[:, j * BLOCK : (j + 1) * BLOCK] = s
                part = fold_max(s)
                top = part if top is None else jnp.maximum(top, part)
            top = jnp.max(top, axis=1, keepdims=True) * (SCALE * LOG2E)
            total = weighted = None
            for j in range(VIS):
                cols = slice(j * BLOCK, (j + 1) * BLOCK)
                e = jnp.exp2(s_ref[:, cols] * (SCALE * LOG2E) - top)
                dp = dot(g[rows], vt[ids[t, j]], 1, 0)
                low = e.astype(bf16)
                e_ref[:, cols] = low
                dp_ref[:, cols] = dp
                e_part, w_part = fold(e), fold(low.astype(f32) * dp)
                total = e_part if total is None else total + e_part
                weighted = w_part if weighted is None else weighted + w_part
            inverse = 1.0 / jnp.sum(total, axis=1, keepdims=True)
            delta = jnp.sum(weighted, axis=1, keepdims=True) * inverse
            across = jnp.broadcast_to(inverse, (ROWS, 128)).T[:1]
            qq = two_parts(q_t[:, rows].astype(f32) * across)
            gg = two_parts(g_t[:, rows].astype(f32) * across)
            for j in range(VIS):
                cols = slice(j * BLOCK, (j + 1) * BLOCK)
                low = e_ref[:, cols]
                ds = (low.astype(f32) * (dp_ref[:, cols] - delta)).astype(bf16)
                ds_ref[:, cols] = ds
                block = ids[t, j]
                part = dot(gg, low, 1, 0)
                dvt[block] += part[:HEAD_DIM] + part[HEAD_DIM:]
                part = dot(qq, ds, 1, 0)
                dkt[block] += (part[:HEAD_DIM] + part[HEAD_DIM:]) * SCALE
            keys = jnp.concatenate([kt[ids[t, j]] for j in range(VIS)], axis=1)
            dq = dot(ds_ref[...], keys, 1, 1)
            dqt[t, :, rows] = (dq * (inverse * SCALE)).T.astype(bf16)
        return None

    lax.fori_loop(0, TILES, tile, None)


def head_grads(ids, kt, vt, qt, gt):
    vmem = pl.BlockSpec(memory_space=pltpu.VMEM)
    wide = VIS * BLOCK
    return pl.pallas_call(
        head_kernel,
        out_shape=[
            jax.ShapeDtypeStruct(qt.shape, bf16),
            jax.ShapeDtypeStruct(kt.shape, f32),
            jax.ShapeDtypeStruct(kt.shape, f32),
        ],
        in_specs=[pl.BlockSpec(memory_space=pltpu.SMEM)] + [vmem] * 4,
        out_specs=[vmem] * 3,
        scratch_shapes=[
            pltpu.VMEM((ROWS, wide), f32),
            pltpu.VMEM((ROWS, wide), bf16),
            pltpu.VMEM((ROWS, wide), f32),
            pltpu.VMEM((ROWS, wide), bf16),
        ],
        compiler_params=pltpu.CompilerParams(vmem_limit_bytes=56 << 20),
    )(ids, kt, vt, qt, gt)


def shift_cam(x, by):
    length = lax.axis_size("cam")
    return lax.ppermute(x, "cam", [(i, (i + by) % length) for i in range(length)])


def local(query, key_img, value_img, d_out, visible):
    cams, bands = lax.axis_size("cam"), lax.axis_size("band")
    cam, band = lax.axis_index("cam"), lax.axis_index("band")
    halves = [[h * HEADS + i for i in range(HEADS)] for h in range(bands // HEADS)]

    def by_head(x):
        return x.reshape(-1, BLOCK, HEADS, HEAD_DIM).transpose(2, 0, 3, 1)

    pairs = jnp.stack([by_head(key_img), by_head(value_img)], axis=1)
    pairs = jnp.concatenate([pairs] * (bands // HEADS), axis=0)
    own = lax.all_to_all(pairs, "band", 0, 0, tiled=True)
    following = shift_cam(own, -1)
    both = jnp.concatenate([own, following], axis=0)
    kt = both[:, 0].reshape(-1, HEAD_DIM, BLOCK)
    vt = both[:, 1].reshape(-1, HEAD_DIM, BLOCK)
    tiles = jnp.stack([by_head(query)[:, 0], by_head(d_out)[:, 0]], axis=1)
    tiles = lax.all_to_all(tiles, "band", 0, 0, tiled=True, axis_index_groups=halves)
    start = cam * bands + band // HEADS * TILES
    ids = lax.dynamic_slice_in_dim(visible, start, TILES, 0)
    per_cam = 2 * bands
    ids = (ids // per_cam - cam) % cams * per_cam + ids % per_cam
    dqt, dkt, dvt = head_grads(ids, kt, vt, tiles[:, 0], tiles[:, 1])
    grads = jnp.stack(
        [x.reshape(2, bands, 2, HEAD_DIM, BLOCK) for x in (dkt, dvt)], axis=2
    )
    came = shift_cam(grads[1].astype(bf16), 1)
    grads = (grads[0] + came.astype(f32)).astype(bf16)
    back = lax.all_to_all(grads, "band", 0, 0, tiled=True)
    back = back.reshape(bands // HEADS, HEADS, 2, 2, HEAD_DIM, BLOCK)
    back = jnp.sum(back.astype(f32), axis=0).astype(bf16)
    back = back.transpose(1, 2, 4, 0, 3).reshape(2, 1, 2 * BLOCK, HEADS * HEAD_DIM)
    dqt = lax.all_to_all(dqt, "band", 0, 0, tiled=True, axis_index_groups=halves)
    d_query = dqt.transpose(2, 0, 1).reshape(BLOCK, HEADS * HEAD_DIM)
    return d_query, back[0], back[1]


def solution(mesh):
    in_specs = (
        P(("cam", "band"), None),
        P("cam", "band", None),
        P("cam", "band", None),
        P(("cam", "band"), None),
        P(),
    )
    out_specs = (P(("cam", "band"), None), P("cam", "band", None), P("cam", "band", None))
    return jax.shard_map(local, mesh=mesh, in_specs=in_specs, out_specs=out_specs, check_vma=False)
```

```python
import functools

import jax
import jax.numpy as jnp
from jax import lax
from jax.experimental import pallas as pl
from jax.experimental.pallas import tpu as pltpu
from jax.sharding import PartitionSpec as P

HEADS = 8
BLOCK = 512
VIS = 6
HEAD_DIM = 32
TILES = 8
BANDS = 16
CAMS = 8
BLOCKS = 2 * BANDS
WIDE = VIS * BLOCK
SCALE = HEAD_DIM**-0.5
LOG2E = 1.4426950408889634
COLS = [slice(j * BLOCK, (j + 1) * BLOCK) for j in range(VIS)]
bf16 = jnp.bfloat16
f32 = jnp.float32


def dot(a, b, contract_a, contract_b):
    return lax.dot_general(
        a, b, (((contract_a,), (contract_b,)), ((), ())), preferred_element_type=f32
    )


def two_parts(x):
    high = x.astype(bf16)
    return jnp.concatenate([high, (x - high.astype(f32)).astype(bf16)], axis=0)


def fold(x, op=jnp.add):
    return functools.reduce(op, [x[:, i : i + 128] for i in range(0, x.shape[1], 128)])


def as_row(x):
    return jnp.broadcast_to(x, (x.shape[0], 128)).T[:1]


def flip(x):
    return x.astype(f32).T.astype(bf16)


def join(old, new, op):
    return new if old is None else op(old, new)


def run_stages(*stages):
    for j in range(VIS):
        for step, _ in stages:
            step(j)
    for _, finish in stages:
        finish()


def loop(low, high, body):
    def step(i, _):
        body(i)
        return None

    lax.fori_loop(low, high, step, None)


def kernel(
    ids, slots, picks, query, key, value, grad,
    d_query, d_key, d_value,
    k_out, v_out, q_out, g_out,
    kt, vt, qt, gt,
    e, s, top, delta, inverse, parts, own,
    n_out, b_out, vn_in, vb_in, kn_in, kb_in,
    dq_out, dq_in,
    k_ss, k_rs, kf_ss, kf_rs, v_ss, v_rs, vf_ss, vf_rs,
    q_ss, q_rs, g_ss, g_rs,
    vn_ss, vn_rs, vb_ss, vb_rs, kn_ss, kn_rs, kb_ss, kb_rs, dq_ss, dq_rs,
):
    cam, band = lax.axis_index("cam"), lax.axis_index("band")
    before = lax.rem(cam + CAMS - 1, CAMS)
    after = lax.rem(cam + 1, CAMS)
    head = lax.rem(band, HEADS)
    first = band - head

    def copy(src, dst, send, recv, **where):
        return pltpu.make_async_remote_copy(
            src_ref=src, dst_ref=dst, send_sem=send, recv_sem=recv,
            device_id=where, device_id_type=pl.DeviceIdType.MESH,
        )

    def ahead(d):
        return lax.rem(band + d, BANDS)

    def behind(d):
        return lax.rem(band + BANDS - d, BANDS)

    barrier = pltpu.get_barrier_semaphore()

    def greet(d):
        pl.semaphore_signal(
            barrier, inc=1, device_id={"band": ahead(d)}, device_id_type=pl.DeviceIdType.MESH
        )

    loop(1, BANDS, greet)
    for other in (before, after):
        pl.semaphore_signal(
            barrier, inc=1, device_id={"cam": other}, device_id_type=pl.DeviceIdType.MESH
        )

    def spread(x, out, held):
        for i in range(2):
            out[:, i] = flip(x[i * BLOCK : (i + 1) * BLOCK]).reshape(HEADS, HEAD_DIM, BLOCK)
        held[pl.ds(2 * band, 2)] = out[head]

    def spread_copy(d, out, held, ss, rs):
        to = ahead(d)
        return copy(
            out.at[lax.rem(to, HEADS)], held.at[pl.ds(2 * band, 2)], ss.at[d], rs.at[band], band=to
        )

    def arrival(d, out, held, ss, rs):
        src = behind(d)
        return copy(out.at[0], held.at[pl.ds(2 * src, 2)], ss.at[d], rs.at[src], band=ahead(d))

    def forward(src, held, ss, rs):
        return copy(
            held.at[pl.ds(2 * src, 2)], held.at[pl.ds(BLOCKS + 2 * src, 2)],
            ss.at[src], rs.at[src], cam=before,
        )

    def relay(d, out, held, ss, rs, fss, frs):
        arrival(d, out, held, ss, rs).wait_recv()
        forward(behind(d), held, fss, frs).start()

    def share(x, out, held):
        out[...] = flip(x[...]).reshape(HEADS, HEAD_DIM, BLOCK)
        held[head] = out[head]

    def share_copy(i, out, held, ss, rs):
        to = lax.rem(head + i, HEADS)
        return copy(out.at[to], held.at[head], ss.at[i], rs.at[head], band=first + to)

    def share_arrival(i, out, held, ss, rs):
        src = lax.rem(head + HEADS - i, HEADS)
        return copy(out.at[0], held.at[src], ss.at[i], rs.at[src], band=first + src)

    k_args = (k_out, kt, k_ss, k_rs)
    v_args = (v_out, vt, v_ss, v_rs)
    q_args = (q_out, qt, q_ss, q_rs)
    g_args = (g_out, gt, g_ss, g_rs)

    spread(key, k_out, kt)
    pl.semaphore_wait(barrier, BANDS + 1)
    loop(1, BANDS, lambda d: spread_copy(d, *k_args).start())
    forward(band, kt, kf_ss, kf_rs).start()
    share(query, q_out, qt)
    loop(1, HEADS, lambda i: share_copy(i, *q_args).start())
    share(grad, g_out, gt)
    spread(value, v_out, vt)
    loop(1, BANDS, lambda d: relay(d, *k_args, kf_ss, kf_rs))
    loop(1, HEADS, lambda i: share_copy(i, *g_args).start())
    loop(1, BANDS, lambda d: spread_copy(d, *v_args).start())
    forward(band, vt, vf_ss, vf_rs).start()
    loop(1, HEADS, lambda i: share_arrival(i, *q_args).wait_recv())
    loop(0, BANDS, lambda src: forward(src, kt, kf_ss, kf_rs).wait_recv())

    def scores(t):
        q = flip(qt[t])
        state = [None]

        def step(j):
            x = dot(q, kt[ids[t, j]], 1, 0)
            s[:, COLS[j]] = x
            state[0] = join(state[0], fold(x, jnp.maximum), jnp.maximum)

        def finish():
            highest = jnp.max(state[0], axis=1, keepdims=True) * (SCALE * LOG2E)
            top[...] = jnp.broadcast_to(highest, (BLOCK, 128))

        return step, finish

    def exponentials(t):
        highest = top[:, :1]
        state = [None]

        def step(j):
            x = jnp.exp2(s[:, COLS[j]] * (SCALE * LOG2E) - highest)
            e[t, :, COLS[j]] = x.astype(bf16)
            state[0] = join(state[0], fold(x), jnp.add)

        def finish():
            inverse[t] = as_row(1.0 / jnp.sum(state[0], axis=1, keepdims=True))

        return step, finish

    def value_parts(t):
        gg = two_parts(gt[t].astype(f32) * inverse[t])

        def step(j):
            x = dot(gg, e[t, :, COLS[j]], 1, 0)
            parts[t, j] = x[:HEAD_DIM] + x[HEAD_DIM:]

        return step, lambda: None

    run_stages(scores(0))
    run_stages(exponentials(0), scores(1))
    loop(1, HEADS, lambda i: share_arrival(i, *g_args).wait_recv())

    def first_pass(p):
        loop(5 * p - 4, 5 * p + 1, lambda d: relay(d, *v_args, vf_ss, vf_rs))
        for t in (2 * p, 2 * p + 1):
            run_stages(exponentials(t - 1), scores(t), value_parts(t - 2))

    loop(1, TILES // 2, first_pass)
    run_stages(exponentials(TILES - 1), value_parts(TILES - 2))
    run_stages(value_parts(TILES - 1))

    def sum_blocks(b, n_out, n_in, ss, rs):
        sums = [None] * 4
        for t in range(TILES):
            x = parts[t, slots[t, b]]
            for c in range(4):
                sums[c] = join(sums[c], x * picks[t, 4 * b + c], jnp.add)
        for c in range(2):
            own[2 * b + c] = sums[c]
            n_out[2 * b + c] = sums[2 + c].astype(bf16)
        next_copy(b, n_out, n_in, ss, rs).start()

    def next_copy(b, n_out, n_in, ss, rs):
        return copy(
            n_out.at[pl.ds(2 * b, 2)], n_in.at[pl.ds(2 * b, 2)], ss.at[b], rs.at[b], cam=after
        )

    def return_copy(to, b_out, b_in, ss, rs):
        return copy(b_out.at[to], b_in.at[band], ss.at[to], rs.at[band], band=to)

    def return_arrival(d, b_out, b_in, ss, rs):
        src = behind(d)
        return copy(b_out.at[src], b_in.at[src], ss.at[src], rs.at[src], band=src)

    def total(b, n_args, b_out):
        next_copy(b, *n_args).wait_recv()
        n_in = n_args[1]
        b_out[b] = (own[pl.ds(2 * b, 2)] + n_in[pl.ds(2 * b, 2)].astype(f32)).astype(bf16)

    def give_back(d, n_args, b_args):
        to = ahead(d)
        total(to, n_args, b_args[0])
        return_copy(to, *b_args).start()

    def keep(n_args, b_out, b_in):
        total(band, n_args, b_out)
        b_in[band] = b_out[band]

    def assemble(b_in, out):
        for i in range(2):
            x = b_in[:HEADS, i].astype(f32) + b_in[HEADS:, i].astype(f32)
            x = x.reshape(HEADS * HEAD_DIM, BLOCK).T
            out[i * BLOCK : (i + 1) * BLOCK] = x.astype(bf16)

    vn_args = (n_out, vn_in, vn_ss, vn_rs)
    vb_args = (b_out, vb_in, vb_ss, vb_rs)
    kn_args = (n_out, kn_in, kn_ss, kn_rs)
    kb_args = (b_out, kb_in, kb_ss, kb_rs)

    loop(0, BANDS, lambda b: sum_blocks(b, *vn_args))
    loop(0, BANDS, lambda src: forward(src, vt, vf_ss, vf_rs).wait_recv())

    def dprobs(t):
        g = flip(gt[t])
        state = [None]

        def step(j):
            x = dot(g, vt[ids[t, j]], 1, 0)
            s[:, COLS[j]] = x
            state[0] = join(state[0], fold(e[t, :, COLS[j]].astype(f32) * x), jnp.add)

        def finish():
            scaled = jnp.broadcast_to(inverse[t], (128, BLOCK)).T
            delta[...] = jnp.sum(state[0], axis=1, keepdims=True) * scaled

        return step, finish

    def key_parts(t):
        qq = two_parts(qt[t].astype(f32) * inverse[t])
        shift = delta[:, :1]

        def step(j):
            ds = e[t, :, COLS[j]] * (s[:, COLS[j]] - shift).astype(bf16)
            x = dot(qq, ds, 1, 0)
            parts[t, j] = (x[:HEAD_DIM] + x[HEAD_DIM:]) * SCALE
            e[t, :, COLS[j]] = ds

        return step, lambda: None

    run_stages(dprobs(0))

    def second_pass(p):
        for t in (2 * p + 1, 2 * p + 2):
            run_stages(key_parts(t - 1), dprobs(t))
        loop(5 * p + 1, 5 * p + 6, lambda d: give_back(d, vn_args, vb_args))

    loop(0, TILES // 2 - 1, second_pass)
    keep(vn_args, b_out, vb_in)
    run_stages(key_parts(TILES - 2), dprobs(TILES - 1))
    run_stages(key_parts(TILES - 1))

    loop(0, BANDS, lambda b: next_copy(b, *vn_args).wait_send())
    loop(0, BANDS, lambda b: sum_blocks(b, *kn_args))

    def query_grad(i):
        t = lax.rem(head + i, HEADS)
        x = None
        for j in range(VIS):
            x = join(x, dot(e[t, :, COLS[j]], kt[ids[t, j]], 1, 1), jnp.add)
        dq_out[t] = (x.T * (inverse[t] * SCALE)).astype(bf16)

    def query_copy(i):
        t = lax.rem(head + i, HEADS)
        return copy(dq_out.at[t], dq_in.at[head], dq_ss.at[i], dq_rs.at[head], band=first + t)

    def query_arrival(i):
        src = lax.rem(head + HEADS - i, HEADS)
        return copy(dq_out.at[src], dq_in.at[src], dq_ss.at[i], dq_rs.at[src], band=first + src)

    def query_step(i):
        query_grad(i)
        query_copy(i).start()

    loop(1, 4, query_step)
    loop(1, BANDS, lambda d: return_copy(ahead(d), *vb_args).wait_send())
    loop(1, 6, lambda d: give_back(d, kn_args, kb_args))
    loop(4, 6, query_step)
    loop(6, 11, lambda d: give_back(d, kn_args, kb_args))
    loop(6, 8, query_step)
    loop(11, 16, lambda d: give_back(d, kn_args, kb_args))
    query_grad(0)
    dq_in[head] = dq_out[head]
    keep(kn_args, b_out, kb_in)

    loop(1, BANDS, lambda d: return_arrival(d, *vb_args).wait_recv())
    assemble(vb_in, d_value)
    loop(1, HEADS, lambda i: query_arrival(i).wait_recv())
    d_query[...] = dq_in[...].reshape(HEADS * HEAD_DIM, BLOCK).astype(f32).T.astype(bf16)
    loop(1, BANDS, lambda d: return_arrival(d, *kb_args).wait_recv())
    assemble(kb_in, d_key)

    def finish_band(d):
        spread_copy(d, *k_args).wait_send()
        spread_copy(d, *v_args).wait_send()
        return_copy(ahead(d), *kb_args).wait_send()

    def finish_cam(b):
        forward(b, kt, kf_ss, kf_rs).wait_send()
        forward(b, vt, vf_ss, vf_rs).wait_send()
        next_copy(b, *kn_args).wait_send()

    def finish_half(i):
        share_copy(i, *q_args).wait_send()
        share_copy(i, *g_args).wait_send()
        query_copy(i).wait_send()

    loop(1, BANDS, finish_band)
    loop(0, BANDS, finish_cam)
    loop(1, HEADS, finish_half)


def attention_grads(ids, slots, picks, query, key, value, grad):
    vmem = pl.BlockSpec(memory_space=pltpu.VMEM)
    smem = pl.BlockSpec(memory_space=pltpu.SMEM)

    def low(*shape):
        return pltpu.VMEM(shape, bf16)

    def full(*shape):
        return pltpu.VMEM(shape, f32)

    piece = (HEAD_DIM, BLOCK)
    dma = pltpu.SemaphoreType.DMA
    return pl.pallas_call(
        kernel,
        out_shape=[
            jax.ShapeDtypeStruct(query.shape, bf16),
            jax.ShapeDtypeStruct(key.shape, bf16),
            jax.ShapeDtypeStruct(value.shape, bf16),
        ],
        in_specs=[smem] * 3 + [vmem] * 4,
        out_specs=[vmem] * 3,
        scratch_shapes=[
            low(HEADS, 2, *piece), low(HEADS, 2, *piece), low(HEADS, *piece), low(HEADS, *piece),
            low(2 * BLOCKS, *piece), low(2 * BLOCKS, *piece), low(TILES, *piece), low(TILES, *piece),
            low(TILES, BLOCK, WIDE), full(BLOCK, WIDE), full(BLOCK, 128), full(BLOCK, 128),
            full(TILES, 1, BLOCK), full(TILES, VIS, *piece), full(BLOCKS, *piece),
        ]
        + [low(BLOCKS, *piece), low(BANDS, 2, *piece)]
        + [low(BLOCKS, *piece), low(BANDS, 2, *piece)] * 2
        + [low(TILES, *piece), low(TILES, *piece)]
        + [dma((BANDS,))] * 8
        + [dma((HEADS,))] * 4
        + [dma((BANDS,))] * 8
        + [dma((HEADS,))] * 2,
        compiler_params=pltpu.CompilerParams(
            collective_id=0, has_side_effects=True, vmem_limit_bytes=62 << 20
        ),
    )(ids, slots, picks, query, key, value, grad)


def local(query, key_img, value_img, d_out, visible):
    cam, band = lax.axis_index("cam"), lax.axis_index("band")
    start = cam * BANDS + band // TILES * TILES
    mine = lax.dynamic_slice_in_dim(visible, start, TILES, 0)
    offset = (mine // BLOCKS - cam) % CAMS
    ids = offset * BLOCKS + mine % BLOCKS
    hit = (mine % BLOCKS // 2)[:, None, :] == jnp.arange(BANDS)[None, :, None]
    slots = jnp.sum(jnp.where(hit, jnp.arange(VIS), 0), axis=2)
    choice = (offset * 2 + mine % 2)[:, None, None, :] == jnp.arange(4)[None, None, :, None]
    picks = jnp.sum((choice & hit[:, :, None]).astype(f32), axis=3).reshape(TILES, 4 * BANDS)
    d_query, d_key, d_value = attention_grads(
        ids, slots, picks, query, key_img[0], value_img[0], d_out
    )
    return d_query, d_key[None], d_value[None]


def solution(mesh):
    in_specs = (
        P(("cam", "band"), None),
        P("cam", "band", None),
        P("cam", "band", None),
        P(("cam", "band"), None),
        P(),
    )
    out_specs = (P(("cam", "band"), None), P("cam", "band", None), P("cam", "band", None))
    return jax.shard_map(local, mesh=mesh, in_specs=in_specs, out_specs=out_specs, check_vma=False)
```

```python
import functools

import jax
import jax.numpy as jnp
from jax import lax
from jax.experimental import pallas as pl
from jax.experimental.pallas import tpu as pltpu
from jax.sharding import PartitionSpec as P

HEADS = 8
BLOCK = 512
VIS = 6
HEAD_DIM = 32
TILES = 8
BANDS = 16
SIDE = 4
CAMS = 8
BLOCKS = 2 * BANDS
WIDE = VIS * BLOCK
SCALE = HEAD_DIM**-0.5
LOG2E = 1.4426950408889634
COLS = [slice(j * BLOCK, (j + 1) * BLOCK) for j in range(VIS)]
bf16 = jnp.bfloat16
f32 = jnp.float32


def dot(a, b, contract_a, contract_b):
    return lax.dot_general(
        a, b, (((contract_a,), (contract_b,)), ((), ())), preferred_element_type=f32
    )


def two_parts(x):
    high = x.astype(bf16)
    return jnp.concatenate([high, (x - high.astype(f32)).astype(bf16)], axis=0)


def fold(x, op=jnp.add):
    return functools.reduce(op, [x[:, i : i + 128] for i in range(0, x.shape[1], 128)])


def as_row(x):
    return jnp.broadcast_to(x, (x.shape[0], 128)).T[:1]


def flip(x):
    return x.astype(f32).T.astype(bf16)


def join(old, new, op):
    return new if old is None else op(old, new)


def run_stages(*stages):
    for j in range(VIS):
        for step, _ in stages:
            step(j)
    for _, finish in stages:
        finish()


def loop(low, high, body):
    def step(i, _):
        body(i)
        return None

    lax.fori_loop(low, high, step, None)


def kernel(
    visible, query, key, value, grad,
    d_query, d_key, d_value,
    k_out, v_out, q_out, g_out,
    kt, vt, qt, gt,
    ids, slots, picks, e, s, top, delta, inverse, parts, own,
    n_out, b_out, vn_in, vb_in, kn_in, kb_in,
    dq_out, dq_in,
    k_ss, k_rs, kf_ss, kf_rs, v_ss, v_rs, vf_ss, vf_rs,
    q_ss, q_rs, g_ss, g_rs,
    vn_ss, vn_rs, vb_ss, vb_rs, kn_ss, kn_rs, kb_ss, kb_rs, dq_ss, dq_rs,
):
    cam, band = lax.axis_index("cam"), lax.axis_index("band")
    before = lax.rem(cam + CAMS - 1, CAMS)
    after = lax.rem(cam + 1, CAMS)
    head = lax.rem(band, HEADS)
    first = band - head

    def copy(src, dst, send, recv, **where):
        return pltpu.make_async_remote_copy(
            src_ref=src, dst_ref=dst, send_sem=send, recv_sem=recv,
            device_id=where, device_id_type=pl.DeviceIdType.MESH,
        )

    def reach(d, sign):
        z, y = lax.div(d, SIDE), lax.rem(d, SIDE)
        z, y = (r + lax.div(r, 2) * (5 - 2 * r) for r in (z, y))
        z = lax.rem(lax.div(band, SIDE) + sign * z + SIDE, SIDE)
        y = lax.rem(lax.rem(band, SIDE) + sign * y + SIDE, SIDE)
        return z * SIDE + y

    def ahead(d):
        return reach(jnp.int32(d), 1)

    def behind(d):
        return reach(jnp.int32(d), -1)

    barrier = pltpu.get_barrier_semaphore()

    def greet(d):
        pl.semaphore_signal(
            barrier, inc=1, device_id={"band": ahead(d)}, device_id_type=pl.DeviceIdType.MESH
        )

    loop(1, BANDS, greet)
    for other in (before, after):
        pl.semaphore_signal(
            barrier, inc=1, device_id={"cam": other}, device_id_type=pl.DeviceIdType.MESH
        )

    def spread(x, out, held):
        for i in range(2):
            out[:, i] = flip(x[i * BLOCK : (i + 1) * BLOCK]).reshape(HEADS, HEAD_DIM, BLOCK)
        held[pl.ds(2 * band, 2)] = out[head]

    def spread_copy(d, out, held, ss, rs):
        to = ahead(d)
        return copy(
            out.at[lax.rem(to, HEADS)], held.at[pl.ds(2 * band, 2)], ss.at[d], rs.at[band], band=to
        )

    def arrival(d, out, held, ss, rs):
        src = behind(d)
        return copy(out.at[0], held.at[pl.ds(2 * src, 2)], ss.at[d], rs.at[src], band=ahead(d))

    def forward(src, held, ss, rs):
        return copy(
            held.at[pl.ds(2 * src, 2)], held.at[pl.ds(BLOCKS + 2 * src, 2)],
            ss.at[src], rs.at[src], cam=before,
        )

    def relay(d, out, held, ss, rs, fss, frs):
        arrival(d, out, held, ss, rs).wait_recv()
        forward(behind(d), held, fss, frs).start()

    def share(x, out, held):
        out[...] = flip(x[...]).reshape(HEADS, HEAD_DIM, BLOCK)
        held[head] = out[head]

    def share_copy(i, out, held, ss, rs):
        to = lax.rem(head + i, HEADS)
        return copy(out.at[to], held.at[head], ss.at[i], rs.at[head], band=first + to)

    def share_arrival(i, out, held, ss, rs):
        src = lax.rem(head + HEADS - i, HEADS)
        return copy(out.at[0], held.at[src], ss.at[i], rs.at[src], band=first + src)

    def make_tables():
        def one_tile(t):
            band_of, choice = [], []
            for j in range(VIS):
                block = visible[cam * BANDS + first + t, j]
                place = lax.rem(block, BLOCKS)
                offset = (lax.div(block, BLOCKS) != cam).astype(jnp.int32)
                ids[t, j] = offset * BLOCKS + place
                band_of.append(lax.div(place, 2))
                choice.append(2 * offset + lax.rem(place, 2))

            def one_band(b):
                hit = [(x == b).astype(jnp.int32) for x in band_of]
                slots[t, b] = functools.reduce(jnp.maximum, [j * hit[j] for j in range(1, VIS)])
                for c in range(4):
                    match = sum(h * (x == c).astype(jnp.int32) for h, x in zip(hit, choice))
                    picks[t, 4 * b + c] = match.astype(f32)

            loop(0, BANDS, one_band)

        loop(0, TILES, one_tile)

    k_args = (k_out, kt, k_ss, k_rs)
    v_args = (v_out, vt, v_ss, v_rs)
    q_args = (q_out, qt, q_ss, q_rs)
    g_args = (g_out, gt, g_ss, g_rs)

    spread(key, k_out, kt)
    pl.semaphore_wait(barrier, BANDS + 1)
    loop(1, BANDS, lambda d: spread_copy(d, *k_args).start())
    forward(band, kt, kf_ss, kf_rs).start()
    share(query, q_out, qt)
    loop(1, HEADS, lambda i: share_copy(i, *q_args).start())
    share(grad, g_out, gt)
    spread(value, v_out, vt)
    loop(1, HEADS, lambda i: share_copy(i, *g_args).start())
    loop(1, BANDS, lambda d: spread_copy(d, *v_args).start())
    forward(band, vt, vf_ss, vf_rs).start()
    make_tables()
    loop(1, BANDS, lambda d: relay(d, *k_args, kf_ss, kf_rs))
    loop(1, HEADS, lambda i: share_arrival(i, *q_args).wait_recv())
    loop(0, BANDS, lambda src: forward(src, kt, kf_ss, kf_rs).wait_recv())

    def scores(t):
        q = flip(qt[t])
        state = [None]

        def step(j):
            x = dot(q, kt[ids[t, j]], 1, 0)
            s[:, COLS[j]] = x
            state[0] = join(state[0], fold(x, jnp.maximum), jnp.maximum)

        def finish():
            highest = jnp.max(state[0], axis=1, keepdims=True) * (SCALE * LOG2E)
            top[...] = jnp.broadcast_to(highest, (BLOCK, 128))

        return step, finish

    def exponentials(t):
        highest = top[:, :1]
        state = [None]

        def step(j):
            x = jnp.exp2(s[:, COLS[j]] * (SCALE * LOG2E) - highest)
            e[t, :, COLS[j]] = x.astype(bf16)
            state[0] = join(state[0], fold(x), jnp.add)

        def finish():
            inverse[t] = as_row(1.0 / jnp.sum(state[0], axis=1, keepdims=True))

        return step, finish

    def value_parts(t):
        gg = two_parts(gt[t].astype(f32) * inverse[t])

        def step(j):
            x = dot(gg, e[t, :, COLS[j]], 1, 0)
            parts[t, j] = x[:HEAD_DIM] + x[HEAD_DIM:]

        return step, lambda: None

    run_stages(scores(0))
    run_stages(exponentials(0), scores(1))
    loop(1, HEADS, lambda i: share_arrival(i, *g_args).wait_recv())

    def first_pass(p):
        for half in range(2):
            t = 2 * p + half
            low = 8 * (p - 1) + 4 * half + 1
            loop(
                jnp.minimum(low, BANDS), jnp.minimum(low + 4, BANDS),
                lambda d: relay(d, *v_args, vf_ss, vf_rs),
            )
            run_stages(exponentials(t - 1), scores(t), value_parts(t - 2))

    loop(1, TILES // 2, first_pass)
    run_stages(exponentials(TILES - 1), value_parts(TILES - 2))
    run_stages(value_parts(TILES - 1))

    def sum_blocks(b, n_out, n_in, ss, rs):
        sums = [None] * 4
        for t in range(TILES):
            x = parts[t, slots[t, b]]
            for c in range(4):
                sums[c] = join(sums[c], x * picks[t, 4 * b + c], jnp.add)
        for c in range(2):
            own[2 * b + c] = sums[c]
            n_out[2 * b + c] = sums[2 + c].astype(bf16)
        next_copy(b, n_out, n_in, ss, rs).start()

    def next_copy(b, n_out, n_in, ss, rs):
        return copy(
            n_out.at[pl.ds(2 * b, 2)], n_in.at[pl.ds(2 * b, 2)], ss.at[b], rs.at[b], cam=after
        )

    def return_copy(to, b_out, b_in, ss, rs):
        return copy(b_out.at[to], b_in.at[band], ss.at[to], rs.at[band], band=to)

    def return_arrival(d, b_out, b_in, ss, rs):
        src = behind(d)
        return copy(b_out.at[src], b_in.at[src], ss.at[src], rs.at[src], band=src)

    def total(b, n_args, b_out):
        next_copy(b, *n_args).wait_recv()
        n_in = n_args[1]
        b_out[b] = (own[pl.ds(2 * b, 2)] + n_in[pl.ds(2 * b, 2)].astype(f32)).astype(bf16)

    def give_back(i, n_args, b_args):
        to = ahead(BANDS - i)
        total(to, n_args, b_args[0])
        return_copy(to, *b_args).start()

    def keep(n_args, b_out, b_in):
        total(band, n_args, b_out)
        b_in[band] = b_out[band]

    def assemble(b_in, out):
        for i in range(2):
            x = b_in[:HEADS, i].astype(f32) + b_in[HEADS:, i].astype(f32)
            x = x.reshape(HEADS * HEAD_DIM, BLOCK).T
            out[i * BLOCK : (i + 1) * BLOCK] = x.astype(bf16)

    vn_args = (n_out, vn_in, vn_ss, vn_rs)
    vb_args = (b_out, vb_in, vb_ss, vb_rs)
    kn_args = (n_out, kn_in, kn_ss, kn_rs)
    kb_args = (b_out, kb_in, kb_ss, kb_rs)

    loop(0, BANDS, lambda i: sum_blocks(ahead(BANDS - 1 - i), *vn_args))
    loop(0, BANDS, lambda src: forward(src, vt, vf_ss, vf_rs).wait_recv())

    def dprobs(t):
        g = flip(gt[t])
        state = [None]

        def step(j):
            x = dot(g, vt[ids[t, j]], 1, 0)
            s[:, COLS[j]] = x
            state[0] = join(state[0], fold(e[t, :, COLS[j]].astype(f32) * x), jnp.add)

        def finish():
            scaled = jnp.broadcast_to(inverse[t], (128, BLOCK)).T
            delta[...] = jnp.sum(state[0], axis=1, keepdims=True) * scaled

        return step, finish

    def key_parts(t):
        qq = two_parts(qt[t].astype(f32) * inverse[t])
        shift = delta[:, :1]

        def step(j):
            ds = e[t, :, COLS[j]] * (s[:, COLS[j]] - shift).astype(bf16)
            x = dot(qq, ds, 1, 0)
            parts[t, j] = (x[:HEAD_DIM] + x[HEAD_DIM:]) * SCALE
            e[t, :, COLS[j]] = ds

        return step, lambda: None

    run_stages(dprobs(0))

    def second_pass(p):
        for t in (2 * p + 1, 2 * p + 2):
            run_stages(key_parts(t - 1), dprobs(t))
        loop(5 * p + 1, 5 * p + 6, lambda d: give_back(d, vn_args, vb_args))

    loop(0, TILES // 2 - 1, second_pass)
    keep(vn_args, b_out, vb_in)
    run_stages(key_parts(TILES - 2), dprobs(TILES - 1))
    run_stages(key_parts(TILES - 1))

    loop(0, BANDS, lambda b: next_copy(b, *vn_args).wait_send())
    loop(0, BANDS, lambda i: sum_blocks(ahead(BANDS - 1 - i), *kn_args))

    def query_grad(i):
        t = lax.rem(head + i, HEADS)
        x = None
        for j in range(VIS):
            x = join(x, dot(e[t, :, COLS[j]], kt[ids[t, j]], 1, 1), jnp.add)
        dq_out[t] = (x.T * (inverse[t] * SCALE)).astype(bf16)

    def query_copy(i):
        t = lax.rem(head + i, HEADS)
        return copy(dq_out.at[t], dq_in.at[head], dq_ss.at[i], dq_rs.at[head], band=first + t)

    def query_arrival(i):
        src = lax.rem(head + HEADS - i, HEADS)
        return copy(dq_out.at[src], dq_in.at[src], dq_ss.at[i], dq_rs.at[src], band=first + src)

    def query_step(i):
        query_grad(i)
        query_copy(i).start()

    loop(1, BANDS, lambda d: return_copy(ahead(d), *vb_args).wait_send())
    loop(1, 4, query_step)

    def query_steps(i):
        query_step(i)
        loop(2 * i - 7, 2 * i - 5, lambda d: give_back(d, kn_args, kb_args))

    loop(4, HEADS, query_steps)
    query_grad(0)
    dq_in[head] = dq_out[head]
    loop(9, BANDS, lambda d: give_back(d, kn_args, kb_args))
    keep(kn_args, b_out, kb_in)

    loop(1, BANDS, lambda d: return_arrival(d, *vb_args).wait_recv())
    assemble(vb_in, d_value)
    loop(1, HEADS, lambda i: query_arrival(i).wait_recv())
    d_query[...] = dq_in[...].reshape(HEADS * HEAD_DIM, BLOCK).astype(f32).T.astype(bf16)
    loop(1, BANDS, lambda d: return_arrival(d, *kb_args).wait_recv())
    assemble(kb_in, d_key)

    def finish_band(d):
        spread_copy(d, *k_args).wait_send()
        spread_copy(d, *v_args).wait_send()
        return_copy(ahead(d), *kb_args).wait_send()

    def finish_cam(b):
        forward(b, kt, kf_ss, kf_rs).wait_send()
        forward(b, vt, vf_ss, vf_rs).wait_send()
        next_copy(b, *kn_args).wait_send()

    def finish_half(i):
        share_copy(i, *q_args).wait_send()
        share_copy(i, *g_args).wait_send()
        query_copy(i).wait_send()

    loop(1, BANDS, finish_band)
    loop(0, BANDS, finish_cam)
    loop(1, HEADS, finish_half)


def attention_grads(visible, query, key, value, grad):
    vmem = pl.BlockSpec(memory_space=pltpu.VMEM)
    smem = pl.BlockSpec(memory_space=pltpu.SMEM)

    def low(*shape):
        return pltpu.VMEM(shape, bf16)

    def full(*shape):
        return pltpu.VMEM(shape, f32)

    piece = (HEAD_DIM, BLOCK)
    dma = pltpu.SemaphoreType.DMA
    return pl.pallas_call(
        kernel,
        out_shape=[
            jax.ShapeDtypeStruct(query.shape, bf16),
            jax.ShapeDtypeStruct(key.shape, bf16),
            jax.ShapeDtypeStruct(value.shape, bf16),
        ],
        in_specs=[smem] + [vmem] * 4,
        out_specs=[vmem] * 3,
        scratch_shapes=[
            low(HEADS, 2, *piece), low(HEADS, 2, *piece), low(HEADS, *piece), low(HEADS, *piece),
            low(2 * BLOCKS, *piece), low(2 * BLOCKS, *piece), low(TILES, *piece), low(TILES, *piece),
            pltpu.SMEM((TILES, VIS), jnp.int32), pltpu.SMEM((TILES, BANDS), jnp.int32),
            pltpu.SMEM((TILES, 4 * BANDS), f32),
            low(TILES, BLOCK, WIDE), full(BLOCK, WIDE), full(BLOCK, 128), full(BLOCK, 128),
            full(TILES, 1, BLOCK), full(TILES, VIS, *piece), full(BLOCKS, *piece),
        ]
        + [low(BLOCKS, *piece), low(BANDS, 2, *piece)]
        + [low(BLOCKS, *piece), low(BANDS, 2, *piece)] * 2
        + [low(TILES, *piece), low(TILES, *piece)]
        + [dma((BANDS,))] * 8
        + [dma((HEADS,))] * 4
        + [dma((BANDS,))] * 8
        + [dma((HEADS,))] * 2,
        compiler_params=pltpu.CompilerParams(
            collective_id=0, has_side_effects=True, vmem_limit_bytes=62 << 20
        ),
    )(visible, query, key, value, grad)


def local(query, key_img, value_img, d_out, visible):
    d_query, d_key, d_value = attention_grads(
        visible, query, key_img[0], value_img[0], d_out
    )
    return d_query, d_key[None], d_value[None]


def solution(mesh):
    in_specs = (
        P(("cam", "band"), None),
        P("cam", "band", None),
        P("cam", "band", None),
        P(("cam", "band"), None),
        P(),
    )
    out_specs = (P(("cam", "band"), None), P("cam", "band", None), P("cam", "band", None))
    return jax.shard_map(local, mesh=mesh, in_specs=in_specs, out_specs=out_specs, check_vma=False)
```

```python
import functools

import jax
import jax.numpy as jnp
from jax import lax
from jax.experimental import pallas as pl
from jax.experimental.pallas import tpu as pltpu
from jax.sharding import PartitionSpec as P

HEADS = 8
BLOCK = 512
VIS = 6
HEAD_DIM = 32
TILES = 8
BANDS = 16
SIDE = 4
CAMS = 8
BLOCKS = 2 * BANDS
WIDE = VIS * BLOCK
SCALE = HEAD_DIM**-0.5
LOG2E = 1.4426950408889634
COLS = [slice(j * BLOCK, (j + 1) * BLOCK) for j in range(VIS)]
bf16 = jnp.bfloat16
f32 = jnp.float32


def dot(a, b, contract_a, contract_b):
    return lax.dot_general(
        a, b, (((contract_a,), (contract_b,)), ((), ())), preferred_element_type=f32
    )


def two_parts(x):
    high = x.astype(bf16)
    return jnp.concatenate([high, (x - high.astype(f32)).astype(bf16)], axis=0)


def fold(x, op=jnp.add):
    return functools.reduce(op, [x[:, i : i + 128] for i in range(0, x.shape[1], 128)])


def as_row(x):
    return jnp.broadcast_to(x, (x.shape[0], 128)).T[:1]


def flip(x):
    return x.astype(f32).T.astype(bf16)


def join(old, new, op):
    return new if old is None else op(old, new)


def run_stages(*stages):
    for j in range(VIS):
        for step, _ in stages:
            step(j)
    for _, finish in stages:
        finish()


def loop(low, high, body):
    def step(i, _):
        body(i)
        return None

    lax.fori_loop(low, high, step, None)


def kernel(
    visible, query_hbm, key_hbm, value_hbm, grad_hbm,
    d_query_hbm, d_key_hbm, d_value_hbm,
    query, key, value, grad, d_query, d_key, d_value, load_sem, store_sem,
    kv_out, q_out, g_out,
    kt, vt, qt, gt,
    ids, slots, picks, e, s, top, delta, inverse, parts, own,
    n_out, b_out, vn_in, vb_in, kn_in, kb_in,
    dq_out, dq_in,
    k_ss, k_rs, kf_ss, kf_rs, v_ss, v_rs, vf_ss, vf_rs,
    q_ss, q_rs, g_ss, g_rs,
    vn_ss, vn_rs, vb_ss, vb_rs, kn_ss, kn_rs, kb_ss, kb_rs, dq_ss, dq_rs,
):
    cam, band = lax.axis_index("cam"), lax.axis_index("band")
    before = lax.rem(cam + CAMS - 1, CAMS)
    after = lax.rem(cam + 1, CAMS)
    head = lax.rem(band, HEADS)
    first = band - head

    def copy(src, dst, send, recv, **where):
        return pltpu.make_async_remote_copy(
            src_ref=src, dst_ref=dst, send_sem=send, recv_sem=recv,
            device_id=where, device_id_type=pl.DeviceIdType.MESH,
        )

    def reach(d, sign):
        z, y = lax.div(d, SIDE), lax.rem(d, SIDE)
        z, y = (r + lax.div(r, 2) * (5 - 2 * r) for r in (z, y))
        z = lax.rem(lax.div(band, SIDE) + sign * z + SIDE, SIDE)
        y = lax.rem(lax.rem(band, SIDE) + sign * y + SIDE, SIDE)
        return z * SIDE + y

    def ahead(d):
        return reach(jnp.int32(d), 1)

    def behind(d):
        return reach(jnp.int32(d), -1)

    def load(i):
        src, dst = ((key_hbm, key), (query_hbm, query), (grad_hbm, grad), (value_hbm, value))[i]
        return pltpu.make_async_copy(src, dst, load_sem.at[i])

    def store(i):
        src, dst = ((d_value, d_value_hbm), (d_query, d_query_hbm), (d_key, d_key_hbm))[i]
        return pltpu.make_async_copy(src, dst, store_sem.at[i])

    def all_done(ref, sem):
        pltpu.make_async_copy(ref, ref, sem.at[0]).wait()

    for i in range(4):
        load(i).start()
    barrier = pltpu.get_barrier_semaphore()

    def greet(d):
        pl.semaphore_signal(
            barrier, inc=1, device_id={"band": ahead(d)}, device_id_type=pl.DeviceIdType.MESH
        )

    loop(1, BANDS, greet)
    for other in (before, after):
        pl.semaphore_signal(
            barrier, inc=1, device_id={"cam": other}, device_id_type=pl.DeviceIdType.MESH
        )

    def spread(x, out, held):
        for i in range(2):
            out[:, i] = flip(x[i * BLOCK : (i + 1) * BLOCK]).reshape(HEADS, HEAD_DIM, BLOCK)
        held[pl.ds(2 * band, 2)] = out[head]

    def spread_copy(d, out, held, ss, rs):
        to = ahead(d)
        return copy(
            out.at[lax.rem(to, HEADS)], held.at[pl.ds(2 * band, 2)], ss.at[0], rs.at[band], band=to
        )

    def arrival(d, out, held, ss, rs):
        src = behind(d)
        return copy(out.at[0], held.at[pl.ds(2 * src, 2)], ss.at[0], rs.at[src], band=ahead(d))

    def forward(src, held, ss, rs):
        return copy(
            held.at[pl.ds(2 * src, 2)], held.at[pl.ds(BLOCKS + 2 * src, 2)],
            ss.at[0], rs.at[0], cam=before,
        )

    def relay(d, out, held, ss, rs, fss, frs):
        arrival(d, out, held, ss, rs).wait_recv()
        forward(behind(d), held, fss, frs).start()

    def share(x, out, held):
        out[...] = flip(x[...]).reshape(HEADS, HEAD_DIM, BLOCK)
        held[head] = out[head]

    def share_copy(i, out, held, ss, rs):
        to = lax.rem(head + i, HEADS)
        return copy(out.at[to], held.at[head], ss.at[0], rs.at[0], band=first + to)

    def make_tables():
        def one_tile(t):
            band_of, choice = [], []
            for j in range(VIS):
                block = visible[j, cam * BANDS + first + t]
                place = lax.rem(block, BLOCKS)
                offset = (lax.div(block, BLOCKS) != cam).astype(jnp.int32)
                ids[t, j] = offset * BLOCKS + place
                band_of.append(lax.div(place, 2))
                choice.append(2 * offset + lax.rem(place, 2))

            def one_band(b):
                hit = [(x == b).astype(jnp.int32) for x in band_of]
                slots[t, b] = functools.reduce(jnp.maximum, [j * hit[j] for j in range(1, VIS)])
                for c in range(4):
                    match = sum(h * (x == c).astype(jnp.int32) for h, x in zip(hit, choice))
                    picks[t, 4 * b + c] = match.astype(f32)

            loop(0, BANDS, one_band)

        loop(0, TILES, one_tile)

    k_out, v_out = kv_out.at[pl.ds(0, HEADS)], kv_out.at[pl.ds(HEADS, HEADS)]
    k_args = (k_out, kt, k_ss, k_rs)
    v_args = (v_out, vt, v_ss, v_rs)
    q_args = (q_out, qt, q_ss, q_rs)
    g_args = (g_out, gt, g_ss, g_rs)

    load(0).wait()
    spread(key, k_out, kt)
    pl.semaphore_wait(barrier, BANDS + 1)
    loop(1, BANDS, lambda d: spread_copy(d, *k_args).start())
    forward(band, kt, kf_ss, kf_rs).start()
    load(1).wait()
    share(query, q_out, qt)
    load(2).wait()
    share(grad, g_out, gt)
    load(3).wait()
    spread(value, v_out, vt)
    make_tables()
    loop(1, 9, lambda d: relay(d, *k_args, kf_ss, kf_rs))
    loop(1, HEADS, lambda i: share_copy(i, *q_args).start())
    loop(1, HEADS, lambda i: share_copy(i, *g_args).start())
    loop(1, BANDS, lambda d: spread_copy(d, *v_args).start())
    forward(band, vt, vf_ss, vf_rs).start()
    loop(9, BANDS, lambda d: relay(d, *k_args, kf_ss, kf_rs))
    all_done(qt.at[pl.ds(0, HEADS - 1)], q_rs)
    all_done(kt.at[pl.ds(0, BLOCKS)], kf_rs)

    def scores(t):
        q = flip(qt[t])
        state = [None]

        def step(j):
            x = dot(q, kt[ids[t, j]], 1, 0)
            s[:, COLS[j]] = x
            state[0] = join(state[0], fold(x, jnp.maximum), jnp.maximum)

        def finish():
            highest = jnp.max(state[0], axis=1, keepdims=True) * (SCALE * LOG2E)
            top[...] = jnp.broadcast_to(highest, (BLOCK, 128))

        return step, finish

    def exponentials(t):
        highest = top[:, :1]
        state = [None]

        def step(j):
            x = jnp.exp2(s[:, COLS[j]] * (SCALE * LOG2E) - highest)
            e[t, :, COLS[j]] = x.astype(bf16)
            state[0] = join(state[0], fold(x), jnp.add)

        def finish():
            inverse[t] = as_row(1.0 / jnp.sum(state[0], axis=1, keepdims=True))

        return step, finish

    def value_parts(t):
        gg = two_parts(gt[t].astype(f32) * inverse[t])

        def step(j):
            x = dot(gg, e[t, :, COLS[j]], 1, 0)
            parts[t, j] = x[:HEAD_DIM] + x[HEAD_DIM:]

        return step, lambda: None

    run_stages(scores(0))
    run_stages(exponentials(0), scores(1))
    all_done(gt.at[pl.ds(0, HEADS - 1)], g_rs)

    def first_pass(p):
        for half in range(2):
            t = 2 * p + half
            low = 8 * (p - 1) + 4 * half + 1
            loop(
                jnp.minimum(low, BANDS), jnp.minimum(low + 4, BANDS),
                lambda d: relay(d, *v_args, vf_ss, vf_rs),
            )
            run_stages(exponentials(t - 1), scores(t), value_parts(t - 2))

    loop(1, TILES // 2, first_pass)
    run_stages(exponentials(TILES - 1), value_parts(TILES - 2))
    run_stages(value_parts(TILES - 1))

    def sum_blocks(b, n_out, n_in, ss, rs):
        sums = [None] * 4
        for t in range(TILES):
            x = parts[t, slots[t, b]]
            for c in range(4):
                sums[c] = join(sums[c], x * picks[t, 4 * b + c], jnp.add)
        for c in range(2):
            own[2 * b + c] = sums[c]
            n_out[2 * b + c] = sums[2 + c].astype(bf16)
        next_copy(b, n_out, n_in, ss, rs).start()

    def next_copy(b, n_out, n_in, ss, rs):
        return copy(
            n_out.at[pl.ds(2 * b, 2)], n_in.at[pl.ds(2 * b, 2)], ss.at[0], rs.at[b], cam=after
        )

    def return_copy(to, b_out, b_in, ss, rs):
        return copy(b_out.at[to], b_in.at[band], ss.at[0], rs.at[0], band=to)

    def total(b, n_args, b_out):
        next_copy(b, *n_args).wait_recv()
        n_in = n_args[1]
        b_out[b] = (own[pl.ds(2 * b, 2)] + n_in[pl.ds(2 * b, 2)].astype(f32)).astype(bf16)

    def give_back(i, n_args, b_args):
        to = ahead(BANDS - i)
        total(to, n_args, b_args[0])
        return_copy(to, *b_args).start()

    def keep(n_args, b_out, b_in):
        total(band, n_args, b_out)
        b_in[band] = b_out[band]

    def assemble(b_in, out):
        for i in range(2):
            x = b_in[:HEADS, i].astype(f32) + b_in[HEADS:, i].astype(f32)
            x = x.reshape(HEADS * HEAD_DIM, BLOCK).T
            out[i * BLOCK : (i + 1) * BLOCK] = x.astype(bf16)

    vn_args = (n_out, vn_in, vn_ss, vn_rs)
    vb_args = (b_out, vb_in, vb_ss, vb_rs)
    kn_args = (n_out, kn_in, kn_ss, kn_rs)
    kb_args = (kv_out, kb_in, kb_ss, kb_rs)

    loop(0, BANDS, lambda i: sum_blocks(ahead(BANDS - 1 - i), *vn_args))
    all_done(vt.at[pl.ds(0, BLOCKS)], vf_rs)
    for sem in (k_ss, v_ss):
        all_done(kt.at[pl.ds(0, BLOCKS - 2)], sem)

    def dprobs(t):
        g = flip(gt[t])
        state = [None]

        def step(j):
            x = dot(g, vt[ids[t, j]], 1, 0)
            s[:, COLS[j]] = x
            state[0] = join(state[0], fold(e[t, :, COLS[j]].astype(f32) * x), jnp.add)

        def finish():
            scaled = jnp.broadcast_to(inverse[t], (128, BLOCK)).T
            delta[...] = jnp.sum(state[0], axis=1, keepdims=True) * scaled

        return step, finish

    def key_parts(t):
        qq = two_parts(qt[t].astype(f32) * inverse[t])
        shift = delta[:, :1]

        def step(j):
            ds = e[t, :, COLS[j]] * (s[:, COLS[j]] - shift).astype(bf16)
            x = dot(qq, ds, 1, 0)
            parts[t, j] = (x[:HEAD_DIM] + x[HEAD_DIM:]) * SCALE
            e[t, :, COLS[j]] = ds

        return step, lambda: None

    run_stages(dprobs(0))

    def second_pass(p):
        for t in (2 * p + 1, 2 * p + 2):
            run_stages(key_parts(t - 1), dprobs(t))
        loop(
            jnp.maximum(8 * p - 7, 1), jnp.minimum(8 * p + 1, BANDS),
            lambda d: give_back(d, vn_args, vb_args),
        )

    loop(0, TILES // 2 - 1, second_pass)
    run_stages(key_parts(TILES - 2), dprobs(TILES - 1))
    run_stages(key_parts(TILES - 1))
    keep(vn_args, b_out, vb_in)
    all_done(n_out, vn_ss)
    loop(0, BANDS, lambda i: sum_blocks(ahead(BANDS - 1 - i), *kn_args))

    def query_grad(i):
        t = lax.rem(head + i, HEADS)
        x = None
        for j in range(VIS):
            x = join(x, dot(e[t, :, COLS[j]], kt[ids[t, j]], 1, 1), jnp.add)
        dq_out[t] = (x.T * (inverse[t] * SCALE)).astype(bf16)

    def query_copy(i):
        t = lax.rem(head + i, HEADS)
        return copy(dq_out.at[t], dq_in.at[head], dq_ss.at[0], dq_rs.at[0], band=first + t)

    def query_step(i):
        query_grad(i)
        query_copy(i).start()

    loop(1, 4, query_step)

    def query_steps(i):
        query_step(i)
        loop(2 * i - 7, 2 * i - 5, lambda d: give_back(d, kn_args, kb_args))

    loop(4, HEADS, query_steps)
    query_grad(0)
    dq_in[head] = dq_out[head]
    loop(9, BANDS, lambda d: give_back(d, kn_args, kb_args))
    keep(kn_args, kv_out, kb_in)

    all_done(vb_in.at[pl.ds(0, BANDS - 1)], vb_rs)
    assemble(vb_in, d_value)
    store(0).start()
    all_done(dq_in.at[pl.ds(0, HEADS - 1)], dq_rs)
    d_query[...] = dq_in[...].reshape(HEADS * HEAD_DIM, BLOCK).astype(f32).T.astype(bf16)
    store(1).start()
    for sem in (kf_ss, vf_ss, kn_ss):
        all_done(kt.at[pl.ds(0, BLOCKS)], sem)
    for sem in (q_ss, g_ss, dq_ss):
        all_done(qt.at[pl.ds(0, HEADS - 1)], sem)
    all_done(kb_in.at[pl.ds(0, BANDS - 1)], kb_rs)
    assemble(kb_in, d_key)
    store(2).start()
    for sem in (vb_ss, kb_ss):
        all_done(b_out.at[pl.ds(0, BANDS - 1)], sem)
    for i in range(3):
        store(i).wait()


def attention_grads(visible, query, key, value, grad):
    hbm = pl.BlockSpec(memory_space=pl.ANY)
    smem = pl.BlockSpec(memory_space=pltpu.SMEM)

    def low(*shape):
        return pltpu.VMEM(shape, bf16)

    def full(*shape):
        return pltpu.VMEM(shape, f32)

    piece = (HEAD_DIM, BLOCK)
    dma = pltpu.SemaphoreType.DMA
    return pl.pallas_call(
        kernel,
        out_shape=[
            jax.ShapeDtypeStruct(query.shape, bf16),
            jax.ShapeDtypeStruct(key.shape, bf16),
            jax.ShapeDtypeStruct(value.shape, bf16),
        ],
        in_specs=[smem] + [hbm] * 4,
        out_specs=[hbm] * 3,
        scratch_shapes=[low(*x.shape) for x in (query, key, value, grad, query, key, value)]
        + [dma((4,)), dma((3,))]
        + [
            low(BANDS, 2, *piece), low(HEADS, *piece), low(HEADS, *piece),
            low(2 * BLOCKS, *piece), low(2 * BLOCKS, *piece), low(TILES, *piece), low(TILES, *piece),
            pltpu.SMEM((TILES, VIS), jnp.int32), pltpu.SMEM((TILES, BANDS), jnp.int32),
            pltpu.SMEM((TILES, 4 * BANDS), f32),
            low(TILES, BLOCK, WIDE), full(BLOCK, WIDE), full(BLOCK, 128), full(BLOCK, 128),
            full(TILES, 1, BLOCK), full(TILES, VIS, *piece), full(BLOCKS, *piece),
        ]
        + [low(BLOCKS, *piece), low(BANDS, 2, *piece)]
        + [low(BLOCKS, *piece), low(BANDS, 2, *piece)] * 2
        + [low(TILES, *piece), low(TILES, *piece)]
        + [dma((n,)) for n in (1, BANDS, 1, 1) * 2 + (1,) * 4 + (1, BANDS, 1, 1) * 2 + (1, 1)],
        compiler_params=pltpu.CompilerParams(
            collective_id=0, has_side_effects=True, vmem_limit_bytes=62 << 20
        ),
    )(visible, query, key, value, grad)


def local(query, key_img, value_img, d_out, visible):
    d_query, d_key, d_value = attention_grads(
        visible.T, query, key_img[0], value_img[0], d_out
    )
    return d_query, d_key[None], d_value[None]


def solution(mesh):
    in_specs = (
        P(("cam", "band"), None),
        P("cam", "band", None),
        P("cam", "band", None),
        P(("cam", "band"), None),
        P(),
    )
    out_specs = (P(("cam", "band"), None), P("cam", "band", None), P("cam", "band", None))
    return jax.shard_map(local, mesh=mesh, in_specs=in_specs, out_specs=out_specs, check_vma=False)
```

```python
import functools

import jax
import jax.numpy as jnp
from jax import lax
from jax.experimental import pallas as pl
from jax.experimental.pallas import tpu as pltpu
from jax.sharding import PartitionSpec as P

HEADS = 8
BLOCK = 512
VIS = 6
HEAD_DIM = 32
TILES = 8
BANDS = 16
SIDE = 4
CAMS = 8
BLOCKS = 2 * BANDS
WIDE = VIS * BLOCK
SCALE = HEAD_DIM**-0.5
LOG2E = 1.4426950408889634
COLS = [slice(j * BLOCK, (j + 1) * BLOCK) for j in range(VIS)]
bf16 = jnp.bfloat16
f32 = jnp.float32


def dot(a, b, contract_a, contract_b):
    return lax.dot_general(
        a, b, (((contract_a,), (contract_b,)), ((), ())), preferred_element_type=f32
    )


def two_parts(x):
    high = x.astype(bf16)
    return jnp.concatenate([high, (x - high.astype(f32)).astype(bf16)], axis=0)


def fold(x, op=jnp.add):
    return functools.reduce(op, [x[:, i : i + 128] for i in range(0, x.shape[1], 128)])


def as_row(x):
    return jnp.broadcast_to(x, (x.shape[0], 128)).T[:1]


def flip(x):
    return x.astype(f32).T.astype(bf16)


def join(old, new, op):
    return new if old is None else op(old, new)


def join_heads(x):
    x = x[:HEADS].astype(f32) + x[HEADS:].astype(f32)
    return x.reshape(HEADS * HEAD_DIM, BLOCK).T.astype(bf16)


def run_stages(*stages):
    for j in range(VIS):
        for step, _ in stages:
            step(j)
    for _, finish in stages:
        finish()


def loop(low, high, body):
    def step(i, _):
        body(i)
        return None

    lax.fori_loop(low, high, step, None)


def kernel(
    visible, query_hbm, key_hbm, value_hbm, grad_hbm,
    d_query_hbm, kb_in, d_value_hbm,
    query, key, value, grad, d_query, d_value, load_sem, store_sem,
    kv_out, q_out, g_out,
    kt, vt, qt, gt,
    ids, slots, picks, e, s, top, delta, inverse, parts, own,
    n_out, b_out, vn_in, vb_in, kn_in,
    dq_out, dq_in,
    k_ss, k_rs, kf_ss, kf_rs, v_ss, v_rs, vf_ss, vf_rs,
    q_ss, q_rs, g_ss, g_rs,
    vn_ss, vn_rs, vb_ss, vb_rs, kn_ss, kn_rs, kb_ss, kb_rs, dq_ss, dq_rs,
):
    cam, band = lax.axis_index("cam"), lax.axis_index("band")
    before = lax.rem(cam + CAMS - 1, CAMS)
    after = lax.rem(cam + 1, CAMS)
    head = lax.rem(band, HEADS)
    first = band - head

    def copy(src, dst, send, recv, **where):
        return pltpu.make_async_remote_copy(
            src_ref=src, dst_ref=dst, send_sem=send, recv_sem=recv,
            device_id=where, device_id_type=pl.DeviceIdType.MESH,
        )

    def reach(d, sign):
        z, y = lax.div(d, SIDE), lax.rem(d, SIDE)
        z, y = (r + lax.div(r, 2) * (5 - 2 * r) for r in (z, y))
        z = lax.rem(lax.div(band, SIDE) + sign * z + SIDE, SIDE)
        y = lax.rem(lax.rem(band, SIDE) + sign * y + SIDE, SIDE)
        return z * SIDE + y

    def ahead(d):
        return reach(jnp.int32(d), 1)

    def behind(d):
        return reach(jnp.int32(d), -1)

    def load(i):
        src, dst = ((key_hbm, key), (query_hbm, query), (grad_hbm, grad), (value_hbm, value))[i]
        return pltpu.make_async_copy(src, dst, load_sem.at[i])

    def store(i):
        src, dst = ((d_value, d_value_hbm), (d_query, d_query_hbm), (kv_out.at[band], kb_in.at[band]))[i]
        return pltpu.make_async_copy(src, dst, store_sem.at[i])

    def all_done(ref, sem):
        pltpu.make_async_copy(ref, ref, sem.at[0]).wait()

    for i in range(4):
        load(i).start()
    barrier = pltpu.get_barrier_semaphore()

    def greet(d):
        pl.semaphore_signal(
            barrier, inc=1, device_id={"band": ahead(d)}, device_id_type=pl.DeviceIdType.MESH
        )

    loop(1, BANDS, greet)
    for other in (before, after):
        pl.semaphore_signal(
            barrier, inc=1, device_id={"cam": other}, device_id_type=pl.DeviceIdType.MESH
        )

    def spread(x, out, held):
        for i in range(2):
            out[:, i] = flip(x[i * BLOCK : (i + 1) * BLOCK]).reshape(HEADS, HEAD_DIM, BLOCK)
        held[pl.ds(2 * band, 2)] = out[head]

    def spread_copy(d, out, held, ss, rs):
        to = ahead(d)
        return copy(
            out.at[lax.rem(to, HEADS)], held.at[pl.ds(2 * band, 2)], ss.at[0], rs.at[band], band=to
        )

    def arrival(d, out, held, ss, rs):
        src = behind(d)
        return copy(out.at[0], held.at[pl.ds(2 * src, 2)], ss.at[0], rs.at[src], band=ahead(d))

    def forward(src, held, ss, rs):
        return copy(
            held.at[pl.ds(2 * src, 2)], held.at[pl.ds(BLOCKS + 2 * src, 2)],
            ss.at[0], rs.at[0], cam=before,
        )

    def relay(d, out, held, ss, rs, fss, frs):
        arrival(d, out, held, ss, rs).wait_recv()
        forward(behind(d), held, fss, frs).start()

    def share(x, out, held):
        out[...] = flip(x[...]).reshape(HEADS, HEAD_DIM, BLOCK)
        held[head] = out[head]

    def share_copy(i, out, held, ss, rs):
        to = lax.rem(head + i, HEADS)
        return copy(out.at[to], held.at[head], ss.at[0], rs.at[0], band=first + to)

    def make_tables():
        def one_tile(t):
            band_of, choice = [], []
            for j in range(VIS):
                block = visible[j, cam * BANDS + first + t]
                place = lax.rem(block, BLOCKS)
                offset = (lax.div(block, BLOCKS) != cam).astype(jnp.int32)
                ids[t, j] = offset * BLOCKS + place
                band_of.append(lax.div(place, 2))
                choice.append(2 * offset + lax.rem(place, 2))

            def one_band(b):
                hit = [(x == b).astype(jnp.int32) for x in band_of]
                slots[t, b] = functools.reduce(jnp.maximum, [j * hit[j] for j in range(1, VIS)])
                for c in range(4):
                    match = sum(h * (x == c).astype(jnp.int32) for h, x in zip(hit, choice))
                    picks[t, 4 * b + c] = match.astype(f32)

            loop(0, BANDS, one_band)

        loop(0, TILES, one_tile)

    k_out, v_out = kv_out.at[pl.ds(0, HEADS)], kv_out.at[pl.ds(HEADS, HEADS)]
    k_args = (k_out, kt, k_ss, k_rs)
    v_args = (v_out, vt, v_ss, v_rs)
    q_args = (q_out, qt, q_ss, q_rs)
    g_args = (g_out, gt, g_ss, g_rs)

    load(0).wait()
    spread(key, k_out, kt)
    pl.semaphore_wait(barrier, BANDS + 1)
    loop(1, BANDS, lambda d: spread_copy(d, *k_args).start())
    forward(band, kt, kf_ss, kf_rs).start()
    load(1).wait()
    share(query, q_out, qt)
    load(2).wait()
    share(grad, g_out, gt)
    load(3).wait()
    spread(value, v_out, vt)
    make_tables()
    loop(1, 9, lambda d: relay(d, *k_args, kf_ss, kf_rs))
    loop(1, HEADS, lambda i: share_copy(i, *q_args).start())
    loop(1, HEADS, lambda i: share_copy(i, *g_args).start())
    loop(1, BANDS, lambda d: spread_copy(d, *v_args).start())
    forward(band, vt, vf_ss, vf_rs).start()
    loop(9, BANDS, lambda d: relay(d, *k_args, kf_ss, kf_rs))
    all_done(qt.at[pl.ds(0, HEADS - 1)], q_rs)
    all_done(kt.at[pl.ds(0, BLOCKS)], kf_rs)

    def scores(t):
        q = flip(qt[t])
        state = [None]

        def step(j):
            x = dot(q, kt[ids[t, j]], 1, 0)
            s[:, COLS[j]] = x
            state[0] = join(state[0], fold(x, jnp.maximum), jnp.maximum)

        def finish():
            highest = jnp.max(state[0], axis=1, keepdims=True) * (SCALE * LOG2E)
            top[...] = jnp.broadcast_to(highest, (BLOCK, 128))

        return step, finish

    def exponentials(t):
        highest = top[:, :1]
        state = [None]

        def step(j):
            x = jnp.exp2(s[:, COLS[j]] * (SCALE * LOG2E) - highest)
            e[t, :, COLS[j]] = x.astype(bf16)
            state[0] = join(state[0], fold(x), jnp.add)

        def finish():
            inverse[t] = as_row(1.0 / jnp.sum(state[0], axis=1, keepdims=True))

        return step, finish

    def value_parts(t):
        gg = two_parts(gt[t].astype(f32) * inverse[t])

        def step(j):
            x = dot(gg, e[t, :, COLS[j]], 1, 0)
            parts[t, j] = x[:HEAD_DIM] + x[HEAD_DIM:]

        return step, lambda: None

    run_stages(scores(0))
    run_stages(exponentials(0), scores(1))
    all_done(gt.at[pl.ds(0, HEADS - 1)], g_rs)

    def first_pass(p):
        for half in range(2):
            t = 2 * p + half
            low = 6 * (p - 1) + 3 * half + 1
            loop(
                jnp.minimum(low, BANDS), jnp.minimum(low + 3, BANDS),
                lambda d: relay(d, *v_args, vf_ss, vf_rs),
            )
            run_stages(exponentials(t - 1), scores(t), value_parts(t - 2))

    loop(1, TILES // 2, first_pass)
    run_stages(exponentials(TILES - 1), value_parts(TILES - 2))
    run_stages(value_parts(TILES - 1))

    def sum_blocks(b, n_out, n_in, ss, rs):
        sums = [None] * 4
        for t in range(TILES):
            x = parts[t, slots[t, b]]
            for c in range(4):
                sums[c] = join(sums[c], x * picks[t, 4 * b + c], jnp.add)
        for c in range(2):
            own[2 * b + c] = sums[c]
            n_out[2 * b + c] = sums[2 + c].astype(bf16)
        next_copy(b, n_out, n_in, ss, rs).start()

    def next_copy(b, n_out, n_in, ss, rs):
        return copy(
            n_out.at[pl.ds(2 * b, 2)], n_in.at[pl.ds(2 * b, 2)], ss.at[0], rs.at[b], cam=after
        )

    def return_copy(to, b_out, b_in, ss, rs):
        return copy(b_out.at[to], b_in.at[band], ss.at[0], rs.at[0], band=to)

    def total(b, n_args, b_out):
        next_copy(b, *n_args).wait_recv()
        n_in = n_args[1]
        b_out[b] = (own[pl.ds(2 * b, 2)] + n_in[pl.ds(2 * b, 2)].astype(f32)).astype(bf16)

    def give_back(i, n_args, b_args):
        to = ahead(BANDS - i)
        total(to, n_args, b_args[0])
        return_copy(to, *b_args).start()

    vn_args = (n_out, vn_in, vn_ss, vn_rs)
    vb_args = (b_out, vb_in, vb_ss, vb_rs)
    kn_args = (n_out, kn_in, kn_ss, kn_rs)
    kb_args = (kv_out, kb_in, kb_ss, kb_rs)

    loop(0, BANDS, lambda i: sum_blocks(ahead(BANDS - 1 - i), *vn_args))
    all_done(vt.at[pl.ds(0, BLOCKS)], vf_rs)
    for sem in (k_ss, v_ss):
        all_done(kt.at[pl.ds(0, BLOCKS - 2)], sem)

    def dprobs(t):
        g = flip(gt[t])
        state = [None]

        def step(j):
            x = dot(g, vt[ids[t, j]], 1, 0)
            s[:, COLS[j]] = x
            state[0] = join(state[0], fold(e[t, :, COLS[j]].astype(f32) * x), jnp.add)

        def finish():
            scaled = jnp.broadcast_to(inverse[t], (128, BLOCK)).T
            delta[...] = jnp.sum(state[0], axis=1, keepdims=True) * scaled

        return step, finish

    def key_parts(t):
        qq = two_parts(qt[t].astype(f32) * inverse[t])
        shift = delta[:, :1]

        def step(j):
            ds = e[t, :, COLS[j]] * (s[:, COLS[j]] - shift).astype(bf16)
            x = dot(qq, ds, 1, 0)
            parts[t, j] = (x[:HEAD_DIM] + x[HEAD_DIM:]) * SCALE
            e[t, :, COLS[j]] = ds

        return step, lambda: None

    run_stages(dprobs(0))

    def second_pass(p):
        for half in range(2):
            t = 2 * p + half + 1
            run_stages(key_parts(t - 1), dprobs(t))
            low = 3 * t - 2
            loop(
                jnp.minimum(low, BANDS), jnp.minimum(low + 3, BANDS),
                lambda i: give_back(i, vn_args, vb_args),
            )

    loop(0, TILES // 2 - 1, second_pass)
    run_stages(key_parts(TILES - 2), dprobs(TILES - 1))
    run_stages(key_parts(TILES - 1))
    total(band, vn_args, b_out)
    vb_in[band] = b_out[band]
    all_done(n_out, vn_ss)
    loop(0, BANDS, lambda i: sum_blocks(ahead(BANDS - 1 - i), *kn_args))

    def query_grad(i):
        t = lax.rem(head + i, HEADS)
        x = None
        for j in range(VIS):
            x = join(x, dot(e[t, :, COLS[j]], kt[ids[t, j]], 1, 1), jnp.add)
        dq_out[t] = (x.T * (inverse[t] * SCALE)).astype(bf16)

    def query_copy(i):
        t = lax.rem(head + i, HEADS)
        return copy(dq_out.at[t], dq_in.at[head], dq_ss.at[0], dq_rs.at[0], band=first + t)

    def query_step(i):
        query_grad(i)
        query_copy(i).start()

    loop(1, 4, query_step)

    def query_steps(i):
        query_step(i)
        loop(2 * i - 7, 2 * i - 5, lambda d: give_back(d, kn_args, kb_args))

    loop(4, HEADS, query_steps)
    query_grad(0)
    dq_in[head] = dq_out[head]
    loop(9, BANDS, lambda d: give_back(d, kn_args, kb_args))
    total(band, kn_args, kv_out)
    store(2).start()

    all_done(vb_in.at[pl.ds(0, BANDS - 1)], vb_rs)
    for i in range(2):
        d_value[i * BLOCK : (i + 1) * BLOCK] = join_heads(vb_in[:, i])
    store(0).start()
    all_done(dq_in.at[pl.ds(0, HEADS - 1)], dq_rs)
    d_query[...] = dq_in[...].reshape(HEADS * HEAD_DIM, BLOCK).astype(f32).T.astype(bf16)
    store(1).start()
    for sem in (kf_ss, vf_ss, kn_ss):
        all_done(kt.at[pl.ds(0, BLOCKS)], sem)
    for sem in (q_ss, g_ss, dq_ss):
        all_done(qt.at[pl.ds(0, HEADS - 1)], sem)
    for sem in (vb_ss, kb_ss, kb_rs):
        all_done(b_out.at[pl.ds(0, BANDS - 1)], sem)
    for i in range(3):
        store(i).wait()


def last_kernel(query_in, sums, value_in, d_query, d_key, d_value):
    for i in range(2):
        d_key[i * BLOCK : (i + 1) * BLOCK] = join_heads(sums[:, i])
    d_query[...] = query_in[...]
    d_value[...] = value_in[...]


def last_step(d_query, sums, d_value):
    vmem = pl.BlockSpec(memory_space=pltpu.VMEM)
    return pl.pallas_call(
        last_kernel,
        out_shape=[jax.ShapeDtypeStruct(x.shape, bf16) for x in (d_query, d_value, d_value)],
        in_specs=[vmem] * 3,
        out_specs=[vmem] * 3,
    )(d_query, sums, d_value)


def attention_grads(visible, query, key, value, grad):
    hbm = pl.BlockSpec(memory_space=pl.ANY)
    smem = pl.BlockSpec(memory_space=pltpu.SMEM)

    def low(*shape):
        return pltpu.VMEM(shape, bf16)

    def full(*shape):
        return pltpu.VMEM(shape, f32)

    piece = (HEAD_DIM, BLOCK)
    dma = pltpu.SemaphoreType.DMA
    return pl.pallas_call(
        kernel,
        out_shape=[
            jax.ShapeDtypeStruct(query.shape, bf16),
            jax.ShapeDtypeStruct((BANDS, 2, *piece), bf16),
            jax.ShapeDtypeStruct(value.shape, bf16),
        ],
        in_specs=[smem] + [hbm] * 4,
        out_specs=[hbm] * 3,
        scratch_shapes=[low(*x.shape) for x in (query, key, value, grad, query, value)]
        + [dma((4,)), dma((3,))]
        + [
            low(BANDS, 2, *piece), low(HEADS, *piece), low(HEADS, *piece),
            low(2 * BLOCKS, *piece), low(2 * BLOCKS, *piece), low(TILES, *piece), low(TILES, *piece),
            pltpu.SMEM((TILES, VIS), jnp.int32), pltpu.SMEM((TILES, BANDS), jnp.int32),
            pltpu.SMEM((TILES, 4 * BANDS), f32),
            low(TILES, BLOCK, WIDE), full(BLOCK, WIDE), full(BLOCK, 128), full(BLOCK, 128),
            full(TILES, 1, BLOCK), full(TILES, VIS, *piece), full(BLOCKS, *piece),
        ]
        + [low(BLOCKS, *piece), low(BANDS, 2, *piece)]
        + [low(BLOCKS, *piece), low(BANDS, 2, *piece), low(BLOCKS, *piece)]
        + [low(TILES, *piece), low(TILES, *piece)]
        + [dma((n,)) for n in (1, BANDS, 1, 1) * 2 + (1,) * 4 + (1, BANDS, 1, 1) * 2 + (1, 1)],
        compiler_params=pltpu.CompilerParams(
            collective_id=0, has_side_effects=True, vmem_limit_bytes=62 << 20
        ),
    )(visible, query, key, value, grad)


def local(query, key_img, value_img, d_out, visible):
    d_query, sums, d_value = attention_grads(visible.T, query, key_img[0], value_img[0], d_out)
    d_query, d_key, d_value = last_step(d_query, sums, d_value)
    return d_query, d_key[None], d_value[None]


def solution(mesh):
    in_specs = (
        P(("cam", "band"), None),
        P("cam", "band", None),
        P("cam", "band", None),
        P(("cam", "band"), None),
        P(),
    )
    out_specs = (P(("cam", "band"), None), P("cam", "band", None), P("cam", "band", None))
    return jax.shard_map(local, mesh=mesh, in_specs=in_specs, out_specs=out_specs, check_vma=False)
```

```python
import functools

import jax
import jax.numpy as jnp
from jax import lax
from jax.experimental import pallas as pl
from jax.experimental.pallas import tpu as pltpu
from jax.sharding import PartitionSpec as P

HEADS = 8
BLOCK = 512
VIS = 6
HEAD_DIM = 32
TILES = 8
BANDS = 16
SIDE = 4
CAMS = 8
BLOCKS = 2 * BANDS
WIDE = VIS * BLOCK
SCALE = HEAD_DIM**-0.5
LOG2E = 1.4426950408889634
COLS = [slice(j * BLOCK, (j + 1) * BLOCK) for j in range(VIS)]
bf16 = jnp.bfloat16
f32 = jnp.float32


def dot(a, b, contract_a, contract_b):
    return lax.dot_general(
        a, b, (((contract_a,), (contract_b,)), ((), ())), preferred_element_type=f32
    )


def two_parts(x):
    high = x.astype(bf16)
    return jnp.concatenate([high, (x - high.astype(f32)).astype(bf16)], axis=0)


def fold(x, op=jnp.add):
    return functools.reduce(op, [x[:, i : i + 128] for i in range(0, x.shape[1], 128)])


def as_row(x):
    return jnp.broadcast_to(x, (x.shape[0], 128)).T[:1]


def flip(x):
    return x.astype(f32).T.astype(bf16)


def join(old, new, op):
    return new if old is None else op(old, new)


def join_heads(x):
    x = x[:HEADS].astype(f32) + x[HEADS:].astype(f32)
    return x.reshape(HEADS * HEAD_DIM, BLOCK).T.astype(bf16)


def run_stages(*stages):
    for j in range(VIS):
        for step, _ in stages:
            step(j)
    for _, finish in stages:
        finish()


def loop(low, high, body):
    def step(i, _):
        body(i)
        return None

    lax.fori_loop(low, high, step, None)


def kernel(
    visible, query_hbm, key_hbm, value_hbm, grad_hbm,
    d_query_hbm, kb_in, d_value_hbm,
    query, key, value, grad, d_query, d_value, load_sem, store_sem,
    kv_out, q_out, g_out,
    kt, vt, qt, gt,
    ids, slots, picks, e, s, top, delta, inverse, parts, own,
    n_out, b_out, vn_in, vb_in, kn_in,
    dq_out, dq_in,
    k_ss, k_rs, kf_ss, kf_rs, v_ss, v_rs, vf_ss, vf_rs,
    q_ss, q_rs, g_ss, g_rs,
    vn_ss, vn_rs, vb_ss, vb_rs, kn_ss, kn_rs, kb_ss, kb_rs, dq_ss, dq_rs,
):
    cam, band = lax.axis_index("cam"), lax.axis_index("band")
    before = lax.rem(cam + CAMS - 1, CAMS)
    after = lax.rem(cam + 1, CAMS)
    head = lax.rem(band, HEADS)
    first = band - head

    def copy(src, dst, send, recv, **where):
        return pltpu.make_async_remote_copy(
            src_ref=src, dst_ref=dst, send_sem=send, recv_sem=recv,
            device_id=where, device_id_type=pl.DeviceIdType.MESH,
        )

    def reach(d, sign):
        z, y = lax.div(d, SIDE), lax.rem(d, SIDE)
        z, y = (r + lax.div(r, 2) * (5 - 2 * r) for r in (z, y))
        z = lax.rem(lax.div(band, SIDE) + sign * z + SIDE, SIDE)
        y = lax.rem(lax.rem(band, SIDE) + sign * y + SIDE, SIDE)
        return z * SIDE + y

    def ahead(d):
        return reach(jnp.int32(d), 1)

    def behind(d):
        return reach(jnp.int32(d), -1)

    def load(i):
        src, dst = ((key_hbm, key), (query_hbm, query), (grad_hbm, grad), (value_hbm, value))[i]
        return pltpu.make_async_copy(src, dst, load_sem.at[i])

    def store(i):
        src, dst = ((d_value, d_value_hbm), (d_query, d_query_hbm), (kv_out.at[band], kb_in.at[band]))[i]
        return pltpu.make_async_copy(src, dst, store_sem.at[i])

    def all_done(ref, sem):
        pltpu.make_async_copy(ref, ref, sem.at[0]).wait()

    for i in range(4):
        load(i).start()
    barrier = pltpu.get_barrier_semaphore()

    def greet(d):
        pl.semaphore_signal(
            barrier, inc=1, device_id={"band": ahead(d)}, device_id_type=pl.DeviceIdType.MESH
        )

    loop(1, BANDS, greet)
    for other in (before, after):
        pl.semaphore_signal(
            barrier, inc=1, device_id={"cam": other}, device_id_type=pl.DeviceIdType.MESH
        )

    def spread(x, out, held):
        for i in range(2):
            out[:, i] = flip(x[i * BLOCK : (i + 1) * BLOCK]).reshape(HEADS, HEAD_DIM, BLOCK)
        held[pl.ds(2 * band, 2)] = out[head]

    def spread_copy(d, out, held, ss, rs):
        to = ahead(d)
        return copy(
            out.at[lax.rem(to, HEADS)], held.at[pl.ds(2 * band, 2)], ss.at[0], rs.at[band], band=to
        )

    def arrival(d, out, held, ss, rs):
        src = behind(d)
        return copy(out.at[0], held.at[pl.ds(2 * src, 2)], ss.at[0], rs.at[src], band=ahead(d))

    def forward(src, held, ss, rs):
        return copy(
            held.at[pl.ds(2 * src, 2)], held.at[pl.ds(BLOCKS + 2 * src, 2)],
            ss.at[0], rs.at[0], cam=before,
        )

    def relay(d, out, held, ss, rs, fss, frs):
        arrival(d, out, held, ss, rs).wait_recv()
        forward(behind(d), held, fss, frs).start()

    def share(x, out, held):
        out[...] = flip(x[...]).reshape(HEADS, HEAD_DIM, BLOCK)
        held[head] = out[head]

    def share_copy(i, out, held, ss, rs):
        to = lax.rem(head + i, HEADS)
        return copy(out.at[to], held.at[head], ss.at[0], rs.at[0], band=first + to)

    def make_tables():
        def one_tile(t):
            band_of, choice = [], []
            for j in range(VIS):
                block = visible[j, cam * BANDS + first + t]
                place = lax.rem(block, BLOCKS)
                offset = (lax.div(block, BLOCKS) != cam).astype(jnp.int32)
                ids[t, j] = offset * BLOCKS + place
                band_of.append(lax.div(place, 2))
                choice.append(2 * offset + lax.rem(place, 2))

            def one_band(b):
                hit = [(x == b).astype(jnp.int32) for x in band_of]
                slots[t, b] = functools.reduce(jnp.maximum, [j * hit[j] for j in range(1, VIS)])
                for c in range(4):
                    match = sum(h * (x == c).astype(jnp.int32) for h, x in zip(hit, choice))
                    picks[t, 4 * b + c] = match.astype(f32)

            loop(0, BANDS, one_band)

        loop(0, TILES, one_tile)

    k_out, v_out = kv_out.at[pl.ds(0, HEADS)], kv_out.at[pl.ds(HEADS, HEADS)]
    k_args = (k_out, kt, k_ss, k_rs)
    v_args = (v_out, vt, v_ss, v_rs)
    q_args = (q_out, qt, q_ss, q_rs)
    g_args = (g_out, gt, g_ss, g_rs)

    load(0).wait()
    spread(key, k_out, kt)
    pl.semaphore_wait(barrier, BANDS + 1)
    loop(1, BANDS, lambda d: spread_copy(d, *k_args).start())
    forward(band, kt, kf_ss, kf_rs).start()
    load(1).wait()
    share(query, q_out, qt)
    load(2).wait()
    share(grad, g_out, gt)
    load(3).wait()
    spread(value, v_out, vt)
    make_tables()
    loop(1, 9, lambda d: relay(d, *k_args, kf_ss, kf_rs))
    loop(1, HEADS, lambda i: share_copy(i, *q_args).start())
    loop(1, HEADS, lambda i: share_copy(i, *g_args).start())
    loop(1, BANDS, lambda d: spread_copy(d, *v_args).start())
    forward(band, vt, vf_ss, vf_rs).start()
    loop(9, BANDS, lambda d: relay(d, *k_args, kf_ss, kf_rs))
    all_done(qt.at[pl.ds(0, HEADS - 1)], q_rs)
    all_done(kt.at[pl.ds(0, BLOCKS)], kf_rs)

    def scores(t):
        q = flip(qt[t])
        state = [None]

        def step(j):
            x = dot(q, kt[ids[t, j]], 1, 0)
            s[:, COLS[j]] = x
            state[0] = join(state[0], fold(x, jnp.maximum), jnp.maximum)

        def finish():
            highest = jnp.max(state[0], axis=1, keepdims=True) * (SCALE * LOG2E)
            top[...] = jnp.broadcast_to(highest, (BLOCK, 128))

        return step, finish

    def exponentials(t):
        highest = top[:, :1]
        state = [None]

        def step(j):
            x = jnp.exp2(s[:, COLS[j]] * (SCALE * LOG2E) - highest)
            e[t, :, COLS[j]] = x.astype(bf16)
            state[0] = join(state[0], fold(x), jnp.add)

        def finish():
            inverse[t] = as_row(1.0 / jnp.sum(state[0], axis=1, keepdims=True))

        return step, finish

    def value_parts(t):
        gg = two_parts(gt[t].astype(f32) * inverse[t])

        def step(j):
            x = dot(gg, e[t, :, COLS[j]], 1, 0)
            parts[t, j] = x[:HEAD_DIM] + x[HEAD_DIM:]

        return step, lambda: None

    run_stages(scores(0))
    run_stages(exponentials(0), scores(1))
    all_done(gt.at[pl.ds(0, HEADS - 1)], g_rs)

    def first_pass(p):
        for half in range(2):
            t = 2 * p + half
            low = 8 * (p - 1) + 4 * half - 3
            loop(
                jnp.clip(low, 1, BANDS), jnp.clip(low + 4, 1, BANDS),
                lambda d: relay(d, *v_args, vf_ss, vf_rs),
            )
            run_stages(exponentials(t - 1), scores(t), value_parts(t - 2))

    loop(1, TILES // 2, first_pass)
    run_stages(exponentials(TILES - 1), value_parts(TILES - 2))
    run_stages(value_parts(TILES - 1))

    def sum_blocks(b, n_out, n_in, ss, rs):
        sums = [None] * 4
        for t in range(TILES):
            x = parts[t, slots[t, b]]
            for c in range(4):
                sums[c] = join(sums[c], x * picks[t, 4 * b + c], jnp.add)
        for c in range(2):
            own[2 * b + c] = sums[c]
            n_out[2 * b + c] = sums[2 + c].astype(bf16)
        next_copy(b, n_out, n_in, ss, rs).start()

    def next_copy(b, n_out, n_in, ss, rs):
        return copy(
            n_out.at[pl.ds(2 * b, 2)], n_in.at[pl.ds(2 * b, 2)], ss.at[0], rs.at[b], cam=after
        )

    def return_copy(to, b_out, b_in, ss, rs):
        return copy(b_out.at[to], b_in.at[band], ss.at[0], rs.at[0], band=to)

    def total(b, n_args, b_out):
        next_copy(b, *n_args).wait_recv()
        n_in = n_args[1]
        b_out[b] = (own[pl.ds(2 * b, 2)] + n_in[pl.ds(2 * b, 2)].astype(f32)).astype(bf16)

    def give_back(i, n_args, b_args):
        to = ahead(BANDS - i)
        total(to, n_args, b_args[0])
        return_copy(to, *b_args).start()

    vn_args = (n_out, vn_in, vn_ss, vn_rs)
    vb_args = (b_out, vb_in, vb_ss, vb_rs)
    kn_args = (n_out, kn_in, kn_ss, kn_rs)
    kb_args = (kv_out, kb_in, kb_ss, kb_rs)

    loop(0, BANDS, lambda i: sum_blocks(ahead(BANDS - 1 - i), *vn_args))
    all_done(vt.at[pl.ds(0, BLOCKS)], vf_rs)
    for sem in (k_ss, v_ss):
        all_done(kt.at[pl.ds(0, BLOCKS - 2)], sem)

    def dprobs(t):
        g = flip(gt[t])
        state = [None]

        def step(j):
            x = dot(g, vt[ids[t, j]], 1, 0)
            s[:, COLS[j]] = x
            state[0] = join(state[0], fold(e[t, :, COLS[j]].astype(f32) * x), jnp.add)

        def finish():
            scaled = jnp.broadcast_to(inverse[t], (128, BLOCK)).T
            delta[...] = jnp.sum(state[0], axis=1, keepdims=True) * scaled

        return step, finish

    def key_parts(t):
        qq = two_parts(qt[t].astype(f32) * inverse[t])
        shift = delta[:, :1]

        def step(j):
            ds = e[t, :, COLS[j]] * (s[:, COLS[j]] - shift).astype(bf16)
            x = dot(qq, ds, 1, 0)
            parts[t, j] = (x[:HEAD_DIM] + x[HEAD_DIM:]) * SCALE
            e[t, :, COLS[j]] = ds

        return step, lambda: None

    late = 1 + (BANDS - 1) * lax.rem(cam, 2)

    def give_range(low, high, n_args, b_args):
        low, high = (jnp.minimum(jnp.maximum(x, late), BANDS) for x in (low, high))
        loop(low, high, lambda i: give_back(i, n_args, b_args))

    loop(1, late, lambda i: give_back(i, vn_args, vb_args))
    run_stages(dprobs(0))

    def second_pass(p):
        for half in range(2):
            t = 2 * p + half + 1
            run_stages(key_parts(t - 1), dprobs(t))
            give_range(3 * t - 2, 3 * t + 1, vn_args, vb_args)

    loop(0, TILES // 2 - 1, second_pass)
    run_stages(key_parts(TILES - 2), dprobs(TILES - 1))
    run_stages(key_parts(TILES - 1))
    total(band, vn_args, b_out)
    vb_in[band] = b_out[band]
    all_done(n_out, vn_ss)
    loop(0, BANDS, lambda i: sum_blocks(ahead(BANDS - 1 - i), *kn_args))

    def query_grad(i):
        t = lax.rem(head + i, HEADS)
        x = None
        for j in range(VIS):
            x = join(x, dot(e[t, :, COLS[j]], kt[ids[t, j]], 1, 1), jnp.add)
        dq_out[t] = (x.T * (inverse[t] * SCALE)).astype(bf16)

    def query_copy(i):
        t = lax.rem(head + i, HEADS)
        return copy(dq_out.at[t], dq_in.at[head], dq_ss.at[0], dq_rs.at[0], band=first + t)

    def query_step(i):
        query_grad(i)
        query_copy(i).start()

    loop(1, late, lambda i: give_back(i, kn_args, kb_args))
    loop(1, 4, query_step)

    def query_steps(i):
        query_step(i)
        give_range(2 * i - 7, 2 * i - 5, kn_args, kb_args)

    loop(4, HEADS, query_steps)
    query_grad(0)
    dq_in[head] = dq_out[head]
    give_range(9, BANDS, kn_args, kb_args)
    total(band, kn_args, kv_out)
    store(2).start()

    all_done(vb_in.at[pl.ds(0, BANDS - 1)], vb_rs)
    for i in range(2):
        d_value[i * BLOCK : (i + 1) * BLOCK] = join_heads(vb_in[:, i])
    store(0).start()
    all_done(dq_in.at[pl.ds(0, HEADS - 1)], dq_rs)
    d_query[...] = dq_in[...].reshape(HEADS * HEAD_DIM, BLOCK).astype(f32).T.astype(bf16)
    store(1).start()
    for sem in (kf_ss, vf_ss, kn_ss):
        all_done(kt.at[pl.ds(0, BLOCKS)], sem)
    for sem in (q_ss, g_ss, dq_ss):
        all_done(qt.at[pl.ds(0, HEADS - 1)], sem)
    for sem in (vb_ss, kb_ss, kb_rs):
        all_done(b_out.at[pl.ds(0, BANDS - 1)], sem)
    for i in range(3):
        store(i).wait()


def last_kernel(query_in, sums, value_in, d_query, d_key, d_value):
    for i in range(2):
        d_key[i * BLOCK : (i + 1) * BLOCK] = join_heads(sums[:, i])
    d_query[...] = query_in[...]
    d_value[...] = value_in[...]


def last_step(d_query, sums, d_value):
    vmem = pl.BlockSpec(memory_space=pltpu.VMEM)
    return pl.pallas_call(
        last_kernel,
        out_shape=[jax.ShapeDtypeStruct(x.shape, bf16) for x in (d_query, d_value, d_value)],
        in_specs=[vmem] * 3,
        out_specs=[vmem] * 3,
    )(d_query, sums, d_value)


def attention_grads(visible, query, key, value, grad):
    hbm = pl.BlockSpec(memory_space=pl.ANY)
    smem = pl.BlockSpec(memory_space=pltpu.SMEM)

    def low(*shape):
        return pltpu.VMEM(shape, bf16)

    def full(*shape):
        return pltpu.VMEM(shape, f32)

    piece = (HEAD_DIM, BLOCK)
    dma = pltpu.SemaphoreType.DMA
    return pl.pallas_call(
        kernel,
        out_shape=[
            jax.ShapeDtypeStruct(query.shape, bf16),
            jax.ShapeDtypeStruct((BANDS, 2, *piece), bf16),
            jax.ShapeDtypeStruct(value.shape, bf16),
        ],
        in_specs=[smem] + [hbm] * 4,
        out_specs=[hbm] * 3,
        scratch_shapes=[low(*x.shape) for x in (query, key, value, grad, query, value)]
        + [dma((4,)), dma((3,))]
        + [
            low(BANDS, 2, *piece), low(HEADS, *piece), low(HEADS, *piece),
            low(2 * BLOCKS, *piece), low(2 * BLOCKS, *piece), low(TILES, *piece), low(TILES, *piece),
            pltpu.SMEM((TILES, VIS), jnp.int32), pltpu.SMEM((TILES, BANDS), jnp.int32),
            pltpu.SMEM((TILES, 4 * BANDS), f32),
            low(TILES, BLOCK, WIDE), full(BLOCK, WIDE), full(BLOCK, 128), full(BLOCK, 128),
            full(TILES, 1, BLOCK), full(TILES, VIS, *piece), full(BLOCKS, *piece),
        ]
        + [low(BLOCKS, *piece), low(BANDS, 2, *piece)]
        + [low(BLOCKS, *piece), low(BANDS, 2, *piece), low(BLOCKS, *piece)]
        + [low(TILES, *piece), low(TILES, *piece)]
        + [dma((n,)) for n in (1, BANDS, 1, 1) * 2 + (1,) * 4 + (1, BANDS, 1, 1) * 2 + (1, 1)],
        compiler_params=pltpu.CompilerParams(
            collective_id=0, has_side_effects=True, vmem_limit_bytes=62 << 20
        ),
    )(visible, query, key, value, grad)


def local(query, key_img, value_img, d_out, visible):
    d_query, sums, d_value = attention_grads(visible.T, query, key_img[0], value_img[0], d_out)
    d_query, d_key, d_value = last_step(d_query, sums, d_value)
    return d_query, d_key[None], d_value[None]


def solution(mesh):
    in_specs = (
        P(("cam", "band"), None),
        P("cam", "band", None),
        P("cam", "band", None),
        P(("cam", "band"), None),
        P(),
    )
    out_specs = (P(("cam", "band"), None), P("cam", "band", None), P("cam", "band", None))
    return jax.shard_map(local, mesh=mesh, in_specs=in_specs, out_specs=out_specs, check_vma=False)
```

```python
import functools

import jax
import jax.numpy as jnp
from jax import lax
from jax.experimental import pallas as pl
from jax.experimental.pallas import tpu as pltpu
from jax.sharding import PartitionSpec as P

HEADS = 8
BLOCK = 512
VIS = 6
HEAD_DIM = 32
TILES = 8
BANDS = 16
SIDE = 4
CAMS = 8
BLOCKS = 2 * BANDS
WIDE = VIS * BLOCK
SCALE = HEAD_DIM**-0.5
LOG2E = 1.4426950408889634
COLS = [slice(j * BLOCK, (j + 1) * BLOCK) for j in range(VIS)]
bf16 = jnp.bfloat16
f32 = jnp.float32


def dot(a, b, contract_a, contract_b):
    return lax.dot_general(
        a, b, (((contract_a,), (contract_b,)), ((), ())), preferred_element_type=f32
    )


def two_parts(x):
    high = x.astype(bf16)
    return jnp.concatenate([high, (x - high.astype(f32)).astype(bf16)], axis=0)


def fold(x, op=jnp.add):
    return functools.reduce(op, [x[:, i : i + 128] for i in range(0, x.shape[1], 128)])


def as_row(x):
    return jnp.broadcast_to(x, (x.shape[0], 128)).T[:1]


def flip(x):
    return x.astype(f32).T.astype(bf16)


def join(old, new, op):
    return new if old is None else op(old, new)


def join_heads(x):
    x = x[:HEADS].astype(f32) + x[HEADS:].astype(f32)
    return x.reshape(HEADS * HEAD_DIM, BLOCK).T.astype(bf16)


def run_stages(*stages):
    for j in range(VIS):
        for step, _ in stages:
            step(j)
    for _, finish in stages:
        finish()


def loop(low, high, body, unroll=1):
    def step(i, _):
        body(i)
        return None

    lax.fori_loop(low, high, step, None, unroll=unroll) if unroll > 1 else lax.fori_loop(low, high, step, None)


def kernel(
    visible, query_hbm, key_hbm, value_hbm, grad_hbm,
    d_query_hbm, kb_in, d_value_hbm,
    query, key, value, grad, d_query, d_value, load_sem, store_sem,
    kv_out, q_out, g_out,
    kt, vt, qt, gt,
    ids, slots, picks, e, s, top, delta, inverse, parts, own,
    n_out, b_out, vn_in, vb_in, kn_in,
    dq_out, dq_in,
    k_ss, k_rs, kf_ss, kf_rs, v_ss, v_rs, vf_ss, vf_rs,
    q_ss, q_rs, g_ss, g_rs,
    vn_ss, vn_rs, vb_ss, vb_rs, kn_ss, kn_rs, kb_ss, kb_rs, dq_ss, dq_rs,
):
    cam, band = lax.axis_index("cam"), lax.axis_index("band")
    before = lax.rem(cam + CAMS - 1, CAMS)
    after = lax.rem(cam + 1, CAMS)
    head = lax.rem(band, HEADS)
    first = band - head

    def copy(src, dst, send, recv, **where):
        return pltpu.make_async_remote_copy(
            src_ref=src, dst_ref=dst, send_sem=send, recv_sem=recv,
            device_id=where, device_id_type=pl.DeviceIdType.MESH,
        )

    def reach(d, sign):
        z, y = lax.div(d, SIDE), lax.rem(d, SIDE)
        z, y = (r + lax.div(r, 2) * (5 - 2 * r) for r in (z, y))
        z = lax.rem(lax.div(band, SIDE) + sign * z + SIDE, SIDE)
        y = lax.rem(lax.rem(band, SIDE) + sign * y + SIDE, SIDE)
        return z * SIDE + y

    def ahead(d):
        return reach(jnp.int32(d), 1)

    def behind(d):
        return reach(jnp.int32(d), -1)

    def load(i):
        src, dst = ((key_hbm, key), (query_hbm, query), (grad_hbm, grad), (value_hbm, value))[i]
        return pltpu.make_async_copy(src, dst, load_sem.at[i])

    def store(i):
        src, dst = ((d_value, d_value_hbm), (d_query, d_query_hbm), (kv_out.at[band], kb_in.at[band]))[i]
        return pltpu.make_async_copy(src, dst, store_sem.at[i])

    def all_done(ref, sem):
        pltpu.make_async_copy(ref, ref, sem.at[0]).wait()

    for i in range(4):
        load(i).start()
    barrier = pltpu.get_barrier_semaphore()

    def greet(d):
        pl.semaphore_signal(
            barrier, inc=1, device_id={"band": ahead(d)}, device_id_type=pl.DeviceIdType.MESH
        )

    loop(1, BANDS, greet)
    for other in (before, after):
        pl.semaphore_signal(
            barrier, inc=1, device_id={"cam": other}, device_id_type=pl.DeviceIdType.MESH
        )

    def spread(x, out, held):
        for i in range(2):
            out[:, i] = flip(x[i * BLOCK : (i + 1) * BLOCK]).reshape(HEADS, HEAD_DIM, BLOCK)
        held[pl.ds(2 * band, 2)] = out[head]

    def spread_copy(d, out, held, ss, rs):
        to = ahead(d)
        return copy(
            out.at[lax.rem(to, HEADS)], held.at[pl.ds(2 * band, 2)], ss.at[0], rs.at[band], band=to
        )

    def arrival(d, out, held, ss, rs):
        src = behind(d)
        return copy(out.at[0], held.at[pl.ds(2 * src, 2)], ss.at[0], rs.at[src], band=ahead(d))

    def forward(src, held, ss, rs):
        return copy(
            held.at[pl.ds(2 * src, 2)], held.at[pl.ds(BLOCKS + 2 * src, 2)],
            ss.at[0], rs.at[0], cam=before,
        )

    def relay(d, out, held, ss, rs, fss, frs):
        arrival(d, out, held, ss, rs).wait_recv()
        forward(behind(d), held, fss, frs).start()

    def share(x, out, held):
        out[...] = flip(x[...]).reshape(HEADS, HEAD_DIM, BLOCK)
        held[head] = out[head]

    def share_copy(i, out, held, ss, rs):
        to = lax.rem(head + i, HEADS)
        return copy(out.at[to], held.at[head], ss.at[0], rs.at[0], band=first + to)

    def make_tables():
        def one_tile(t):
            band_of, choice = [], []
            for j in range(VIS):
                block = visible[j, cam * BANDS + first + t]
                place = lax.rem(block, BLOCKS)
                offset = (lax.div(block, BLOCKS) != cam).astype(jnp.int32)
                ids[t, j] = offset * BLOCKS + place
                band_of.append(lax.div(place, 2))
                choice.append(2 * offset + lax.rem(place, 2))

            def one_band(b):
                hit = [(x == b).astype(jnp.int32) for x in band_of]
                slots[t, b] = functools.reduce(jnp.maximum, [j * hit[j] for j in range(1, VIS)])
                for c in range(4):
                    match = sum(h * (x == c).astype(jnp.int32) for h, x in zip(hit, choice))
                    picks[t, 4 * b + c] = match.astype(f32)

            loop(0, BANDS, one_band)

        loop(0, TILES, one_tile)

    k_out, v_out = kv_out.at[pl.ds(0, HEADS)], kv_out.at[pl.ds(HEADS, HEADS)]
    k_args = (k_out, kt, k_ss, k_rs)
    v_args = (v_out, vt, v_ss, v_rs)
    q_args = (q_out, qt, q_ss, q_rs)
    g_args = (g_out, gt, g_ss, g_rs)

    load(0).wait()
    spread(key, k_out, kt)
    pl.semaphore_wait(barrier, BANDS + 1)
    loop(1, BANDS, lambda d: spread_copy(d, *k_args).start())
    forward(band, kt, kf_ss, kf_rs).start()
    load(1).wait()
    share(query, q_out, qt)
    load(2).wait()
    share(grad, g_out, gt)
    load(3).wait()
    spread(value, v_out, vt)
    make_tables()
    loop(1, 9, lambda d: relay(d, *k_args, kf_ss, kf_rs))
    loop(1, HEADS, lambda i: share_copy(i, *q_args).start())
    loop(1, HEADS, lambda i: share_copy(i, *g_args).start())
    loop(1, BANDS, lambda d: spread_copy(d, *v_args).start())
    forward(band, vt, vf_ss, vf_rs).start()
    loop(9, BANDS, lambda d: relay(d, *k_args, kf_ss, kf_rs))
    all_done(qt.at[pl.ds(0, HEADS - 1)], q_rs)
    all_done(kt.at[pl.ds(0, BLOCKS)], kf_rs)

    def scores(t):
        q = flip(qt[t])
        state = [None]

        def step(j):
            x = dot(q, kt[ids[t, j]], 1, 0)
            s[:, COLS[j]] = x
            state[0] = join(state[0], fold(x, jnp.maximum), jnp.maximum)

        def finish():
            highest = jnp.max(state[0], axis=1, keepdims=True) * (SCALE * LOG2E)
            top[...] = jnp.broadcast_to(highest, (BLOCK, 128))

        return step, finish

    def exponentials(t):
        highest = top[:, :1]
        state = [None]

        def step(j):
            x = jnp.exp2(s[:, COLS[j]] * (SCALE * LOG2E) - highest)
            e[t, :, COLS[j]] = x.astype(bf16)
            state[0] = join(state[0], fold(x), jnp.add)

        def finish():
            inverse[t] = as_row(1.0 / jnp.sum(state[0], axis=1, keepdims=True))

        return step, finish

    def value_parts(t):
        gg = two_parts(gt[t].astype(f32) * inverse[t])

        def step(j):
            x = dot(gg, e[t, :, COLS[j]], 1, 0)
            parts[t, j] = x[:HEAD_DIM] + x[HEAD_DIM:]

        return step, lambda: None

    run_stages(scores(0))
    run_stages(exponentials(0), scores(1))
    all_done(gt.at[pl.ds(0, HEADS - 1)], g_rs)

    def first_pass(p):
        for half in range(2):
            t = 2 * p + half
            low = 8 * (p - 1) + 4 * half - 3
            loop(
                jnp.clip(low, 1, BANDS), jnp.clip(low + 4, 1, BANDS),
                lambda d: relay(d, *v_args, vf_ss, vf_rs),
            )
            run_stages(exponentials(t - 1), scores(t), value_parts(t - 2))

    loop(1, TILES // 2, first_pass)
    run_stages(exponentials(TILES - 1), value_parts(TILES - 2))
    run_stages(value_parts(TILES - 1))

    def sum_blocks(b, n_out, n_in, ss, rs):
        sums = [None] * 4
        for t in range(TILES):
            x = parts[t, slots[t, b]]
            for c in range(4):
                sums[c] = join(sums[c], x * picks[t, 4 * b + c], jnp.add)
        for c in range(2):
            own[2 * b + c] = sums[c]
            n_out[2 * b + c] = sums[2 + c].astype(bf16)
        next_copy(b, n_out, n_in, ss, rs).start()

    def next_copy(b, n_out, n_in, ss, rs):
        return copy(
            n_out.at[pl.ds(2 * b, 2)], n_in.at[pl.ds(2 * b, 2)], ss.at[0], rs.at[b], cam=after
        )

    def return_copy(to, b_out, b_in, ss, rs):
        return copy(b_out.at[to], b_in.at[band], ss.at[0], rs.at[0], band=to)

    def total(b, n_args, b_out):
        next_copy(b, *n_args).wait_recv()
        n_in = n_args[1]
        b_out[b] = (own[pl.ds(2 * b, 2)] + n_in[pl.ds(2 * b, 2)].astype(f32)).astype(bf16)

    def give_back(i, n_args, b_args):
        to = ahead(BANDS - i)
        total(to, n_args, b_args[0])
        return_copy(to, *b_args).start()

    vn_args = (n_out, vn_in, vn_ss, vn_rs)
    vb_args = (b_out, vb_in, vb_ss, vb_rs)
    kn_args = (n_out, kn_in, kn_ss, kn_rs)
    kb_args = (kv_out, kb_in, kb_ss, kb_rs)

    loop(0, BANDS, lambda i: sum_blocks(ahead(BANDS - 1 - i), *vn_args), 4)
    all_done(vt.at[pl.ds(0, BLOCKS)], vf_rs)
    for sem in (k_ss, v_ss):
        all_done(kt.at[pl.ds(0, BLOCKS - 2)], sem)

    def dprobs(t):
        g = flip(gt[t])
        state = [None]

        def step(j):
            x = dot(g, vt[ids[t, j]], 1, 0)
            s[:, COLS[j]] = x
            state[0] = join(state[0], fold(e[t, :, COLS[j]].astype(f32) * x), jnp.add)

        def finish():
            scaled = jnp.broadcast_to(inverse[t], (128, BLOCK)).T
            delta[...] = jnp.sum(state[0], axis=1, keepdims=True) * scaled

        return step, finish

    def key_parts(t):
        qq = two_parts(qt[t].astype(f32) * inverse[t])
        shift = delta[:, :1]

        def step(j):
            ds = e[t, :, COLS[j]] * (s[:, COLS[j]] - shift).astype(bf16)
            x = dot(qq, ds, 1, 0)
            parts[t, j] = (x[:HEAD_DIM] + x[HEAD_DIM:]) * SCALE
            e[t, :, COLS[j]] = ds

        return step, lambda: None

    late = 1 + (BANDS - 1) * lax.rem(cam, 2)

    def give_range(low, high, n_args, b_args):
        low, high = (jnp.minimum(jnp.maximum(x, late), BANDS) for x in (low, high))
        loop(low, high, lambda i: give_back(i, n_args, b_args))

    loop(1, late, lambda i: give_back(i, vn_args, vb_args))
    run_stages(dprobs(0))

    def second_pass(p):
        for half in range(2):
            t = 2 * p + half + 1
            run_stages(key_parts(t - 1), dprobs(t))
            give_range(3 * t - 2, 3 * t + 1, vn_args, vb_args)

    loop(0, TILES // 2 - 1, second_pass)
    run_stages(key_parts(TILES - 2), dprobs(TILES - 1))
    run_stages(key_parts(TILES - 1))
    total(band, vn_args, b_out)
    vb_in[band] = b_out[band]
    all_done(n_out, vn_ss)
    loop(0, BANDS, lambda i: sum_blocks(ahead(BANDS - 1 - i), *kn_args), 4)

    def query_grad(i):
        t = lax.rem(head + i, HEADS)
        x = None
        for j in range(VIS):
            x = join(x, dot(e[t, :, COLS[j]], kt[ids[t, j]], 1, 1), jnp.add)
        dq_out[t] = (x.T * (inverse[t] * SCALE)).astype(bf16)

    def query_copy(i):
        t = lax.rem(head + i, HEADS)
        return copy(dq_out.at[t], dq_in.at[head], dq_ss.at[0], dq_rs.at[0], band=first + t)

    def query_step(i):
        query_grad(i)
        query_copy(i).start()

    loop(1, late, lambda i: give_back(i, kn_args, kb_args))
    loop(1, 4, query_step)

    def query_steps(i):
        query_step(i)
        give_range(2 * i - 7, 2 * i - 5, kn_args, kb_args)

    loop(4, HEADS, query_steps)
    query_grad(0)
    dq_in[head] = dq_out[head]
    give_range(9, BANDS, kn_args, kb_args)
    total(band, kn_args, kv_out)
    store(2).start()

    all_done(vb_in.at[pl.ds(0, BANDS - 1)], vb_rs)
    for i in range(2):
        d_value[i * BLOCK : (i + 1) * BLOCK] = join_heads(vb_in[:, i])
    store(0).start()
    all_done(dq_in.at[pl.ds(0, HEADS - 1)], dq_rs)
    d_query[...] = dq_in[...].reshape(HEADS * HEAD_DIM, BLOCK).astype(f32).T.astype(bf16)
    store(1).start()
    for sem in (kf_ss, vf_ss, kn_ss):
        all_done(kt.at[pl.ds(0, BLOCKS)], sem)
    for sem in (q_ss, g_ss, dq_ss):
        all_done(qt.at[pl.ds(0, HEADS - 1)], sem)
    for sem in (vb_ss, kb_ss, kb_rs):
        all_done(b_out.at[pl.ds(0, BANDS - 1)], sem)
    for i in range(3):
        store(i).wait()


def last_kernel(query_in, sums, value_in, d_query, d_key, d_value):
    for i in range(2):
        d_key[i * BLOCK : (i + 1) * BLOCK] = join_heads(sums[:, i])
    d_query[...] = query_in[...]
    d_value[...] = value_in[...]


def last_step(d_query, sums, d_value):
    vmem = pl.BlockSpec(memory_space=pltpu.VMEM)
    return pl.pallas_call(
        last_kernel,
        out_shape=[jax.ShapeDtypeStruct(x.shape, bf16) for x in (d_query, d_value, d_value)],
        in_specs=[vmem] * 3,
        out_specs=[vmem] * 3,
    )(d_query, sums, d_value)


def attention_grads(visible, query, key, value, grad):
    hbm = pl.BlockSpec(memory_space=pl.ANY)
    smem = pl.BlockSpec(memory_space=pltpu.SMEM)

    def low(*shape):
        return pltpu.VMEM(shape, bf16)

    def full(*shape):
        return pltpu.VMEM(shape, f32)

    piece = (HEAD_DIM, BLOCK)
    dma = pltpu.SemaphoreType.DMA
    return pl.pallas_call(
        kernel,
        out_shape=[
            jax.ShapeDtypeStruct(query.shape, bf16),
            jax.ShapeDtypeStruct((BANDS, 2, *piece), bf16),
            jax.ShapeDtypeStruct(value.shape, bf16),
        ],
        in_specs=[smem] + [hbm] * 4,
        out_specs=[hbm] * 3,
        scratch_shapes=[low(*x.shape) for x in (query, key, value, grad, query, value)]
        + [dma((4,)), dma((3,))]
        + [
            low(BANDS, 2, *piece), low(HEADS, *piece), low(HEADS, *piece),
            low(2 * BLOCKS, *piece), low(2 * BLOCKS, *piece), low(TILES, *piece), low(TILES, *piece),
            pltpu.SMEM((TILES, VIS), jnp.int32), pltpu.SMEM((TILES, BANDS), jnp.int32),
            pltpu.SMEM((TILES, 4 * BANDS), f32),
            low(TILES, BLOCK, WIDE), full(BLOCK, WIDE), full(BLOCK, 128), full(BLOCK, 128),
            full(TILES, 1, BLOCK), full(TILES, VIS, *piece), full(BLOCKS, *piece),
        ]
        + [low(BLOCKS, *piece), low(BANDS, 2, *piece)]
        + [low(BLOCKS, *piece), low(BANDS, 2, *piece), low(BLOCKS, *piece)]
        + [low(TILES, *piece), low(TILES, *piece)]
        + [dma((n,)) for n in (1, BANDS, 1, 1) * 2 + (1,) * 4 + (1, BANDS, 1, 1) * 2 + (1, 1)],
        compiler_params=pltpu.CompilerParams(
            collective_id=0, has_side_effects=True, vmem_limit_bytes=62 << 20
        ),
    )(visible, query, key, value, grad)


def local(query, key_img, value_img, d_out, visible):
    d_query, sums, d_value = attention_grads(visible.T, query, key_img[0], value_img[0], d_out)
    d_query, d_key, d_value = last_step(d_query, sums, d_value)
    return d_query, d_key[None], d_value[None]


def solution(mesh):
    in_specs = (
        P(("cam", "band"), None),
        P("cam", "band", None),
        P("cam", "band", None),
        P(("cam", "band"), None),
        P(),
    )
    out_specs = (P(("cam", "band"), None), P("cam", "band", None), P("cam", "band", None))
    return jax.shard_map(local, mesh=mesh, in_specs=in_specs, out_specs=out_specs, check_vma=False)
```
